512 devices in a mesh: fsdp: 16 (over y, core), tok: 32 (over x, z).
Axes of the slice: x: 4, y: 8, z: 8, core: 2. Of those that a mesh axis runs over, the one named last changes fastest.
Arguments:
- embedded_pieces: bfloat16 [16, 4096, 1024], P('fsdp', 'tok'), may hold values from -6 to 6
- morton_arrangement: int32 [16, 32, 128], P('fsdp', 'tok'), may hold values from 0 to 127, each once within a row
- unhidden_indicator: int32 [16, 4096], P('fsdp'), may hold values 0 or 1
- bordering_tiles: int32 [16, 64, 4], P('fsdp'), may hold values from 0 to 63, as said below
- bordering_tally: int32 [16, 64], P('fsdp'), may hold values from 3 to 4
- standardizer_multiplier: bfloat16 [1024], replicated, may hold values from 0.099609375 to 1.8984375
- sharpness_coefficient: float32 [8], replicated, may hold values from 2 to 12
- probe_projector: bfloat16 [1024, 512], P('fsdp'), may hold values from -0.1875 to 0.1875
- lookup_projector: bfloat16 [1024, 512], P('fsdp'), may hold values from -0.1875 to 0.1875
- content_projector: bfloat16 [1024, 512], P('fsdp'), may hold values from -0.75 to 0.75
- result_projector: bfloat16 [512, 1024], P(None, 'fsdp'), may hold values from -0.25 to 0.25
- upstream_derivative: bfloat16 [16, 4096, 1024], P('fsdp', 'tok'), may hold values from -6 to 6
Outputs:
- layer_out: bfloat16 [16, 4096, 1024], P('fsdp', 'tok')
- grad_tokens: bfloat16 [16, 4096, 1024], P('fsdp', 'tok')
The draws below stay inside these ranges and needn't reach their ends.
Inputs may be any that keep to these rules, and one draw needn't show every extreme that they name: `morton_arrangement`: each row is an order of the positions 0 to 127 of one device. `bordering_tiles`: a block's neighbours lie on other devices than its own (device = block // 2); the 8 entries of one device's blocks are distinct blocks, at most 1 of them on any one device, and exactly 1 on some device.
All inputs are finite; a program needn't handle non-finite values. No bound on the sum of `unhidden_indicator` on one device may be relied on, other than what follows from the above.
Results may differ from the reference program's by a relative error of at most 0.0092.
Values may be sent and summed in bfloat16 or wider, within the bound.
No kernel may reach another device: no remote copies, remote signals or barrier semaphores. Data moves between devices by JAX's collectives and lax.ppermute only.
A program may use at most 64 MiB of HBM per device.

```python
import math
import jax
import jax.numpy as jnp
from jax import lax

D = 1024
NEARBY_ATTN_SETS = 8
HEAD_DIM = 64
BLOCK = 64
KN = 4
TOK_DEV = 128
HDT = 512
NB = 2
SHARDS = 32
SCENES = 16
SCENE_TOK = 4096
SCENE_BLOCKS = 64
CAP = 1


def device_lists(device_key, device):
    keys_all = jax.random.split(device_key, 4)
    requests = NB * KN
    others = (device + 1 + jax.random.permutation(keys_all[0], SHARDS - 1)) % SHARDS
    pool = jax.random.permutation(keys_all[1], (SHARDS - 2) * CAP)[:requests - CAP]
    pool_device = others[1 + pool // CAP]
    pool_slot = pool % CAP
    source = jnp.concatenate([jnp.full((CAP,), others[0]), pool_device]).astype(jnp.int32)
    slot_number = jnp.concatenate([jnp.arange(CAP), pool_slot]).astype(jnp.int32)
    offsets = jax.random.randint(keys_all[2], (SHARDS,), 0, NB)
    block_local = (offsets[source] + slot_number) % NB
    shuffle = jax.random.permutation(keys_all[3], requests)
    chosen = (source * NB + block_local)[shuffle]
    return chosen.reshape(NB, KN).astype(jnp.int32)


def scene_lists(scene_key):
    device_keys = jax.random.split(scene_key, SHARDS)
    devices_all = jnp.arange(SHARDS, dtype=jnp.int32)
    per_device = jax.vmap(device_lists)(device_keys, devices_all)
    return per_device.reshape(SCENE_BLOCKS, KN)


def draw_bordering_tiles(key, part):
    scene_keys = jax.random.split(jax.random.fold_in(key, 17), SCENES)
    return jax.vmap(scene_lists)(scene_keys).astype(jnp.int32)


def place_ends(drawn, own_key, low, high):
    shape = drawn.shape
    place = [jax.random.randint(jax.random.fold_in(own_key, axis), (), 0, shape[axis]) for axis in range(len(shape))]
    drawn = drawn.at[tuple(place)].set(low)
    longest = shape.index(max(shape))
    place[longest] = (place[longest] + 1) % shape[longest]
    return drawn.at[tuple(place)].set(high)


def shard_levels(key, extent, pieces, smallest, top_value):
    level = 1.0
    for dim, blocks in pieces:
        heights = jax.random.uniform(jax.random.fold_in(jax.random.fold_in(key, 6), dim), (blocks,), jnp.float32, smallest / len(pieces), top_value / len(pieces))
        level = level * jnp.repeat(jnp.exp(heights), extent[dim] // blocks).reshape((-1,) + (1,) * (len(extent) - 1 - dim))
    return level


def gaussian(stream_key, shape, spread, most, cuts=(), kind=jnp.bfloat16):
    entries = jax.random.normal(stream_key, shape, jnp.float32) * spread
    if len(cuts) > 0:
        entries = shard_levels(stream_key, shape, cuts, -0.22, 0.18) * entries
    return jnp.clip(entries, min=-most, max=most).astype(kind)


def setup_inputs(seed: int = 0) -> dict:
    arg_keys = jax.random.split(jax.random.key(seed), 13)
    return {
        "embedded_pieces": gaussian(arg_keys[0], (SCENES, SCENE_TOK, D), 1.0, 6.0, ((0, 16), (1, 32))),
        "morton_arrangement": jax.vmap(lambda own: jax.random.permutation(own, TOK_DEV))(jax.random.split(arg_keys[1], SCENES * SHARDS)).reshape((SCENES, SHARDS, TOK_DEV)).astype(jnp.int32),
        "unhidden_indicator": place_ends((jax.random.randint(arg_keys[2], (SCENES, SCENE_TOK), 0, 5) < 2).astype(jnp.int32), jax.random.fold_in(arg_keys[2], 1), 0, 1),
        "bordering_tiles": draw_bordering_tiles(jax.random.fold_in(arg_keys[12], 71), 0),
        "bordering_tally": place_ends(jax.random.randint(arg_keys[4], (SCENES, SCENE_BLOCKS), 3, KN + 1), jax.random.fold_in(arg_keys[4], 1), 3, KN).astype(jnp.int32),
        "standardizer_multiplier": jnp.clip(1.0 + 0.18 * jax.random.normal(arg_keys[5], (D,), jnp.float32), 0.099609375, 1.8984375).astype(jnp.bfloat16),
        "sharpness_coefficient": jnp.clip(jnp.exp(jax.random.uniform(arg_keys[6], (NEARBY_ATTN_SETS,), jnp.float32, math.log(2.0), math.log(12.0))), 2.0, 12.0),
        "probe_projector": gaussian(arg_keys[7], (D, HDT), D ** -0.5, 0.1875, ((0, 16),)),
        "lookup_projector": gaussian(arg_keys[8], (D, HDT), D ** -0.5, 0.1875, ((0, 16),)),
        "content_projector": gaussian(arg_keys[9], (D, HDT), (D // 16) ** -0.5, 0.75, ((0, 16),)),
        "result_projector": gaussian(arg_keys[10], (HDT, D), HDT ** -0.5, 0.25, ((1, 16),)),
        "upstream_derivative": gaussian(arg_keys[11], (SCENES, SCENE_TOK, D), 1.0, 6.0, ((0, 16), (1, 32))),
    }


norm_eps = 1e-05
head_eps = 1e-06

def split_heads(matrix):
    return matrix.reshape(matrix.shape[:-1] + (NEARBY_ATTN_SETS, HEAD_DIM))

def inverse_norm(matrix):
    values = matrix.astype(jnp.float32)
    return 1.0 / jnp.sqrt(lax.optimization_barrier(jnp.sum(values * values, axis=-1)) + head_eps)

def lone_sample(embedded_pieces, morton_arrangement, unhidden_indicator, bordering_tiles, bordering_tally, upstream_derivative, standardizer_multiplier, sharpness_coefficient, probe_projector, lookup_projector, content_projector, result_projector):
    per_peer = TOK_DEV // SHARDS
    key_count = (1 + KN) * BLOCK
    shard_rows = embedded_pieces.reshape(SHARDS, TOK_DEV, D)
    arranged = jnp.take_along_axis(shard_rows, morton_arrangement[:, :, None].astype(jnp.int32), axis=1)
    grouped = arranged.reshape(SHARDS, SHARDS, per_peer, D).transpose(1, 0, 2, 3).reshape(SCENE_TOK, D)
    grouped_f = grouped.astype(jnp.float32)
    centered = grouped_f - lax.optimization_barrier(jnp.mean(grouped_f, axis=-1, keepdims=True))
    inv_std = 1.0 / jnp.sqrt(lax.optimization_barrier(jnp.mean(centered * centered, axis=-1, keepdims=True)) + norm_eps)
    normed = centered * inv_std
    gain_f = standardizer_multiplier.astype(jnp.float32)
    normalized = (normed * gain_f).astype(jnp.bfloat16)
    queries = jnp.dot(normalized, probe_projector, preferred_element_type=jnp.float32).astype(jnp.bfloat16)
    key_rows = jnp.dot(normalized, lookup_projector, preferred_element_type=jnp.float32).astype(jnp.bfloat16)
    value_rows = jnp.dot(normalized, content_projector, preferred_element_type=jnp.float32).astype(jnp.bfloat16)
    query_heads = split_heads(queries).reshape(SCENE_BLOCKS, BLOCK, NEARBY_ATTN_SETS, HEAD_DIM)
    key_blocks = split_heads(key_rows).reshape(SCENE_BLOCKS, BLOCK, NEARBY_ATTN_SETS, HEAD_DIM)
    value_blocks = split_heads(value_rows).reshape(SCENE_BLOCKS, BLOCK, NEARBY_ATTN_SETS, HEAD_DIM)
    lists = bordering_tiles.astype(jnp.int32)
    key_all = jnp.concatenate([key_blocks[:, None], key_blocks[lists]], axis=1).reshape(SCENE_BLOCKS, key_count, NEARBY_ATTN_SETS, HEAD_DIM)
    value_all = jnp.concatenate([value_blocks[:, None], value_blocks[lists]], axis=1).reshape(SCENE_BLOCKS, key_count, NEARBY_ATTN_SETS, HEAD_DIM)
    seen = unhidden_indicator.reshape(SCENE_BLOCKS, BLOCK) > 0
    in_use = jnp.arange(KN)[None, :] < bordering_tally[:, None]
    own_allowed = seen[:, None, :] | jnp.eye(BLOCK, dtype=bool)[None]
    tile_allowed = (seen[lists] & in_use[:, :, None]).reshape(SCENE_BLOCKS, 1, KN * BLOCK)
    tile_allowed = jnp.broadcast_to(tile_allowed, (SCENE_BLOCKS, BLOCK, KN * BLOCK))
    allowed = jnp.concatenate([own_allowed, tile_allowed], axis=-1)
    reciprocal_probe_length = inverse_norm(query_heads)
    reciprocal_lookup_length = inverse_norm(key_all)
    multiplier_amount = sharpness_coefficient[None, :, None, None] * jnp.transpose(reciprocal_probe_length, (0, 2, 1))[..., None] * jnp.transpose(reciprocal_lookup_length, (0, 2, 1))[:, :, None, :]
    query_f = query_heads.astype(jnp.float32)
    key_f = key_all.astype(jnp.float32)
    value_f = value_all.astype(jnp.float32)
    raw = jnp.einsum('bihd,bjhd->bhij', query_f, key_f)
    scores = multiplier_amount * raw
    expo = jnp.where(allowed[:, None], jnp.exp(scores), 0.0)
    prob = expo / lax.optimization_barrier(jnp.sum(expo, axis=-1, keepdims=True))
    prob_b = prob.astype(jnp.bfloat16)
    attended = jnp.einsum('bhij,bjhd->bihd', prob_b.astype(jnp.float32), value_f).astype(jnp.bfloat16)
    attended = attended.reshape(SCENE_TOK, HDT)
    layer_out = (grouped_f + jnp.dot(attended, result_projector, preferred_element_type=jnp.float32)).astype(jnp.bfloat16)
    grad_attn = jnp.dot(upstream_derivative, result_projector.T, preferred_element_type=jnp.float32).astype(jnp.bfloat16)
    grad_heads = split_heads(grad_attn).reshape(SCENE_BLOCKS, BLOCK, NEARBY_ATTN_SETS, HEAD_DIM).astype(jnp.float32)
    dprob = jnp.einsum('bihd,bjhd->bhij', grad_heads, value_f)
    delta = lax.optimization_barrier(jnp.sum(prob * dprob, axis=-1, keepdims=True))
    dscore = prob * (dprob - delta)
    weighted = (multiplier_amount * dscore).astype(jnp.bfloat16).astype(jnp.float32)
    score_grad = scores * dscore
    row_terms = jnp.transpose(lax.optimization_barrier(jnp.sum(score_grad, axis=-1)), (0, 2, 1))
    col_terms = jnp.transpose(lax.optimization_barrier(jnp.sum(score_grad, axis=2)), (0, 2, 1))
    grad_query = jnp.einsum('bhij,bjhd->bihd', weighted, key_f) - (reciprocal_probe_length * reciprocal_probe_length * row_terms)[..., None] * query_f
    grad_query = grad_query.astype(jnp.bfloat16).reshape(SCENE_TOK, HDT)
    key_part = jnp.einsum('bhij,bihd->bjhd', weighted, query_f) - (reciprocal_lookup_length * reciprocal_lookup_length * col_terms)[..., None] * key_f
    value_part = jnp.einsum('bhij,bihd->bjhd', prob_b.astype(jnp.float32), grad_heads)
    key_part = key_part.reshape(SCENE_BLOCKS, 1 + KN, BLOCK, HDT)
    value_part = value_part.reshape(SCENE_BLOCKS, 1 + KN, BLOCK, HDT)
    tile_part = jnp.concatenate([key_part[:, 1:], value_part[:, 1:]], axis=-1).astype(jnp.bfloat16)
    remote = jax.ops.segment_sum(tile_part.reshape(SCENE_BLOCKS * KN, BLOCK, 2 * HDT).astype(jnp.float32), lists.reshape(-1), num_segments=SCENE_BLOCKS)
    grad_key = (key_part[:, 0] + remote[..., :HDT]).astype(jnp.bfloat16).reshape(SCENE_TOK, HDT)
    grad_value = (value_part[:, 0] + remote[..., HDT:]).astype(jnp.bfloat16).reshape(SCENE_TOK, HDT)
    grad_hidden = jnp.dot(grad_query, probe_projector.T, preferred_element_type=jnp.float32)
    grad_hidden = grad_hidden + jnp.dot(grad_key, lookup_projector.T, preferred_element_type=jnp.float32)
    grad_hidden = grad_hidden + jnp.dot(grad_value, content_projector.T, preferred_element_type=jnp.float32)
    grad_normed = grad_hidden * gain_f
    grad_grouped = upstream_derivative.astype(jnp.float32) + inv_std * (grad_normed - lax.optimization_barrier(jnp.mean(grad_normed, axis=-1, keepdims=True)) - normed * lax.optimization_barrier(jnp.mean(grad_normed * normed, axis=-1, keepdims=True)))
    grad_grouped = grad_grouped.astype(jnp.bfloat16)
    by_source = grad_grouped.reshape(SHARDS, SHARDS, per_peer, D).transpose(1, 0, 2, 3).reshape(SHARDS, TOK_DEV, D)
    source_index = jnp.arange(SHARDS, dtype=jnp.int32)[:, None]
    grad_tokens = jnp.zeros((SHARDS, TOK_DEV, D), jnp.bfloat16).at[source_index, morton_arrangement.astype(jnp.int32)].set(by_source)
    return (layer_out, grad_tokens.reshape(SCENE_TOK, D))

def reference(embedded_pieces, morton_arrangement, unhidden_indicator, bordering_tiles, bordering_tally, standardizer_multiplier, sharpness_coefficient, probe_projector, lookup_projector, content_projector, result_projector, upstream_derivative):

    def run(sample_parameters):
        return lone_sample(*sample_parameters, standardizer_multiplier, sharpness_coefficient, probe_projector, lookup_projector, content_projector, result_projector)
    layer_out, grad_tokens = lax.map(run, (embedded_pieces, morton_arrangement, unhidden_indicator, bordering_tiles, bordering_tally, upstream_derivative))
    return (layer_out, grad_tokens)
```

```python
import jax
import jax.numpy as jnp
from jax import lax
from jax.experimental import pallas as pl
from jax.experimental.pallas import tpu as pltpu
from jax.sharding import PartitionSpec as P

HEADS = 8
HEAD_DIM = 64
BLOCK = 64
KN = 4
D = 1024
HDT = 512
SHARDS = 32
TOK = 128
NB = 2
CHUNK = 4
SLOTS = 1 + KN
ITEMS = NB * SLOTS
ROWS = ITEMS * BLOCK
KEYS = SLOTS * BLOCK
HALF = D // 2
PACK = ITEMS * CHUNK
GROUP = 4
GL = GROUP * HEAD_DIM
GR = GROUP * BLOCK

norm_eps = 1e-05
head_eps = 1e-06
F32 = jnp.float32
BF16 = jnp.bfloat16
VM = pl.BlockSpec(memory_space=pltpu.VMEM)
SM = pl.BlockSpec(memory_space=pltpu.SMEM)
NN = (((1,), (0,)), ((), ()))
NT = (((1,), (1,)), ((), ()))
TN = (((0,), (0,)), ((), ()))


def dot(a, b, dims, **kw):
    return lax.dot_general(a, b, dims, preferred_element_type=F32, **kw)


def one_hot(row_ref, rows):
    idx = row_ref[...]
    iota = lax.broadcasted_iota(jnp.int32, (rows, idx.shape[1]), 0)
    return jnp.where(iota == idx, 1.0, 0.0).astype(BF16)


def arrange_kernel(side_ref, order_ref, x_ref, keep_ref, send_ref):
    a = dot(one_hot(order_ref, TOK), x_ref[...], TN).astype(BF16)
    lower = side_ref[0] == 0
    left, right = a[:, :HALF], a[:, HALF:]
    keep_ref[...] = jnp.where(lower, left, right)
    send_ref[...] = jnp.where(lower, right, left)


def pack_kernel(side_ref, target_ref, keep_ref, recv_ref, out_ref):
    lower = side_ref[0] == 0
    keep, recv = keep_ref[...], recv_ref[...]
    table = jnp.concatenate(
        [jnp.where(lower, keep, recv), jnp.where(lower, recv, keep)], axis=0
    )
    out_ref[...] = dot(one_hot(target_ref, 2 * TOK), table, TN).astype(BF16)


def collect_kernel(side_ref, target_ref, in_ref, keep_ref, send_ref):
    total = dot(one_hot(target_ref, 2 * TOK), in_ref[...], NN).astype(BF16)
    lower = side_ref[0] == 0
    even, odd = total[:TOK], total[TOK:]
    keep_ref[...] = jnp.where(lower, even, odd)
    send_ref[...] = jnp.where(lower, odd, even)


def restore_kernel(side_ref, order_ref, keep_ref, recv_ref, out_ref):
    lower = side_ref[0] == 0
    keep, recv = keep_ref[...], recv_ref[...]
    both = jnp.concatenate(
        [jnp.where(lower, keep, recv), jnp.where(lower, recv, keep)], axis=1
    )
    out_ref[...] = dot(one_hot(order_ref, TOK), both, NN).astype(BF16)


def main_kernel(
    sharp_ref,
    in_ref,
    perm_ref,
    back_ref,
    w_ref,
    up_ref,
    gain_ref,
    seen_ref,
    out_ref,
    att_ref,
    own_ref,
    normed_ref,
    rstd_ref,
    xn_ref,
    k_ref,
    v_ref,
    gkv_ref,
    gq_ref,
    gh_ref,
):
    x_in = jnp.concatenate([in_ref[:ROWS], in_ref[ROWS:]], axis=1)
    normed_ref[...] = dot(perm_ref[...], x_in, NN)
    gain = gain_ref[...].astype(F32)
    for t in range(ITEMS):
        rows = pl.ds(t * BLOCK, BLOCK)
        x = normed_ref[rows, :]
        if t % SLOTS == 0:
            own_ref[pl.ds(t // SLOTS * BLOCK, BLOCK), :] = x.astype(BF16)
        centered = x - jnp.mean(x, axis=1, keepdims=True)
        rstd = 1.0 / jnp.sqrt(jnp.mean(centered * centered, axis=1, keepdims=True) + norm_eps)
        normed = centered * rstd
        normed_ref[rows, :] = normed
        rstd_ref[rows, :] = jnp.broadcast_to(rstd, (BLOCK, 128))
        xn_ref[rows, :] = (normed * gain).astype(BF16)
    xn = xn_ref[...]
    k_ref[...] = dot(xn, w_ref[:, HDT : 2 * HDT], NN).astype(BF16)
    v_ref[...] = dot(xn, w_ref[:, 2 * HDT : 3 * HDT], NN).astype(BF16)
    xn_own = jnp.concatenate([xn_ref[pl.ds(b * KEYS, BLOCK), :] for b in range(NB)], axis=0)
    queries = dot(xn_own, w_ref[:, :HDT], NN).astype(BF16)
    grad_attn = dot(up_ref[...], w_ref[:, 3 * HDT :], NN).astype(BF16)

    lane_head = lax.broadcasted_iota(jnp.int32, (BLOCK, GL), 1) // HEAD_DIM
    head_pick = (
        lax.broadcasted_iota(jnp.int32, (HEADS, HDT), 1) // HEAD_DIM
        == lax.broadcasted_iota(jnp.int32, (HEADS, HDT), 0)
    ).astype(F32)
    group_pick = (
        lax.broadcasted_iota(jnp.int32, (8, GL), 1) // HEAD_DIM
        == lax.broadcasted_iota(jnp.int32, (8, GL), 0)
    ).astype(F32)
    diagonal = lax.broadcasted_iota(jnp.int32, (BLOCK, KEYS), 0) == lax.broadcasted_iota(
        jnp.int32, (BLOCK, KEYS), 1
    )

    def spread(m):
        return jnp.concatenate(
            [jnp.where(lane_head == h, m, jnp.zeros_like(m)) for h in range(GROUP)], axis=0
        )

    def gather_heads(m):
        total = jnp.where(lane_head == 0, m[:BLOCK], 0.0)
        for h in range(1, GROUP):
            total = jnp.where(lane_head == h, m[h * BLOCK : (h + 1) * BLOCK], total)
        return total

    for b in range(NB):
        keys = pl.ds(b * KEYS, KEYS)
        own = slice(b * BLOCK, (b + 1) * BLOCK)
        kf = k_ref[keys, :].astype(F32)
        norm2 = dot(head_pick, kf * kf, NT, precision=lax.Precision.HIGHEST)
        inv_k = 1.0 / jnp.sqrt(norm2 + head_eps)
        allowed = (seen_ref[b : b + 1, :] > 0.0) | diagonal
        mask = jnp.concatenate([allowed] * GROUP, axis=0)
        for g in range(HEADS // GROUP):
            lanes = slice(g * GL, (g + 1) * GL)
            qm = spread(queries[own, lanes])
            gm = spread(grad_attn[own, lanes])
            k4 = k_ref[keys, lanes]
            v4 = v_ref[keys, lanes]
            qf = qm.astype(F32)
            inv_q = 1.0 / jnp.sqrt(jnp.sum(qf * qf, axis=1, keepdims=True) + head_eps)
            sharp = jnp.concatenate(
                [jnp.full((BLOCK, 1), sharp_ref[g * GROUP + h], F32) for h in range(GROUP)], axis=0
            )
            ik = inv_k[g * GROUP : (g + 1) * GROUP]
            ik_rows = jnp.concatenate(
                [jnp.broadcast_to(ik[h : h + 1], (BLOCK, KEYS)) for h in range(GROUP)], axis=0
            )
            factor = (sharp * inv_q) * ik_rows
            scores = factor * dot(qm, k4, NT)
            expo = jnp.where(mask, jnp.exp(scores), 0.0)
            prob = expo * (1.0 / jnp.sum(expo, axis=1, keepdims=True))
            prob_b = prob.astype(BF16)
            att_ref[own, lanes] = gather_heads(dot(prob_b, v4, NN)).astype(BF16)
            dprob = dot(gm, v4, NT)
            delta = jnp.sum(prob * dprob, axis=1, keepdims=True)
            dscore = prob * (dprob - delta)
            weighted = (factor * dscore).astype(BF16)
            score_grad = scores * dscore
            row_terms = jnp.sum(score_grad, axis=1, keepdims=True)
            gq = dot(weighted, k4, NN) - (inv_q * inv_q * row_terms) * qf
            gq_ref[own, lanes] = gather_heads(gq).astype(BF16)
            col_terms = jnp.concatenate(
                [
                    jnp.sum(score_grad[h * BLOCK : (h + 1) * BLOCK], axis=0, keepdims=True)
                    for h in range(GROUP)
                ],
                axis=0,
            )
            coef = ik * ik * col_terms
            coef = jnp.concatenate([coef, jnp.zeros_like(coef)], axis=0)
            coef = dot(coef, group_pick, TN, precision=lax.Precision.HIGHEST)
            gk = dot(weighted, qm, TN) - coef * k4.astype(F32)
            gkv_ref[keys, g * GL : (g + 1) * GL] = gk.astype(BF16)
            gkv_ref[keys, HDT + g * GL : HDT + (g + 1) * GL] = dot(prob_b, gm, TN).astype(BF16)

    gh_ref[...] = dot(gkv_ref[...], w_ref[:, HDT : 3 * HDT], NT)
    gq_hidden = dot(gq_ref[...], w_ref[:, :HDT], NT)
    for t in range(ITEMS):
        rows = pl.ds(t * BLOCK, BLOCK)
        hidden = gh_ref[rows, :]
        b = t // SLOTS
        if t % SLOTS == 0:
            hidden = hidden + gq_hidden[b * BLOCK : (b + 1) * BLOCK]
        grad = hidden * gain
        normed = normed_ref[rows, :]
        m1 = jnp.mean(grad, axis=1, keepdims=True)
        m2 = jnp.mean(grad * normed, axis=1, keepdims=True)
        grad = rstd_ref[rows, 0:1] * (grad - m1 - normed * m2)
        if t % SLOTS == 0:
            grad = grad + up_ref[pl.ds(b * BLOCK, BLOCK), :].astype(F32)
        xn_ref[rows, :] = grad.astype(BF16)
    back = dot(back_ref[...], xn_ref[...], NN).astype(BF16)
    out_ref[:ROWS] = back[:, :HALF]
    out_ref[ROWS:] = back[:, HALF:]


def output_kernel(att_ref, own_ref, w_ref, out_ref):
    out_ref[...] = (
        own_ref[...].astype(F32) + dot(att_ref[...], w_ref[:, 3 * HDT :], NT)
    ).astype(BF16)


def call(kernel, outs, args, specs, flops, scratch=(), limit=16):
    outs = [jax.ShapeDtypeStruct(shape, BF16) for shape in outs]
    moved = sum(a.size * a.dtype.itemsize for a in list(args) + outs)
    return pl.pallas_call(
        kernel,
        out_shape=outs,
        in_specs=specs,
        out_specs=[VM] * len(outs),
        scratch_shapes=list(scratch),
        compiler_params=pltpu.CompilerParams(vmem_limit_bytes=limit * 2**20),
        cost_estimate=pl.CostEstimate(flops=flops, bytes_accessed=moved, transcendentals=0),
    )(*args)


def body(
    embedded_pieces,
    morton_arrangement,
    unhidden_indicator,
    bordering_tiles,
    bordering_tally,
    standardizer_multiplier,
    sharpness_coefficient,
    probe_projector,
    lookup_projector,
    content_projector,
    result_projector,
    upstream_derivative,
):
    me = lax.axis_index("tok")
    side = (me // (SHARDS // 2)).reshape(1).astype(jnp.int32)
    partner = [(i, i ^ (SHARDS // 2)) for i in range(SHARDS)]
    shares = jnp.concatenate(
        [probe_projector, lookup_projector, content_projector, result_projector.T], axis=1
    )
    weights = lax.all_gather(shares, "fsdp", axis=0, tiled=True)

    order = morton_arrangement[0]
    keep, send = call(
        arrange_kernel,
        [(TOK, HALF)] * 2,
        (side, order, embedded_pieces[0]),
        [SM, VM, VM],
        2 * TOK * TOK * D,
    )
    recv = lax.ppermute(send, "tok", partner)

    lists = bordering_tiles[0].reshape(SHARDS, NB, KN)
    own_blocks = jnp.arange(SHARDS * NB, dtype=jnp.int32).reshape(SHARDS, NB, 1)
    named = jnp.concatenate([own_blocks, lists], axis=2).reshape(SHARDS, ITEMS)
    target = (named % 2) * TOK + (named // 2) * CHUNK
    target = (target[:, :, None] + jnp.arange(CHUNK, dtype=jnp.int32)).reshape(
        1, SHARDS * PACK
    )
    (packed,) = call(
        pack_kernel,
        [(SHARDS * PACK, HALF)],
        (side, target, keep, recv),
        [SM, VM, VM, VM],
        2 * SHARDS * PACK * 2 * TOK * HALF,
    )
    arrived = lax.all_to_all(
        packed.reshape(SHARDS, PACK, HALF), "tok", split_axis=0, concat_axis=0, tiled=True
    ).reshape(SHARDS * PACK, HALF)

    seen_all = unhidden_indicator[0].reshape(SHARDS * NB, BLOCK).astype(F32)
    used = jnp.arange(SLOTS)[None, :] <= bordering_tally[0][:, None]
    used = used.reshape(SHARDS, ITEMS)
    picks = (
        (named[:, :, None] == jnp.arange(SHARDS * NB)) & used[:, :, None]
    ).astype(F32)
    picks = jnp.sum(picks * (jnp.arange(SHARDS) == me)[:, None, None], axis=0)
    seen = jnp.dot(picks, seen_all).reshape(NB, KEYS)

    dest = jnp.arange(ROWS)
    source = (dest % BLOCK // CHUNK) * PACK + (dest // BLOCK) * CHUNK + dest % CHUNK
    perm = (source[:, None] == jnp.arange(ROWS)[None, :]).astype(BF16)
    back = (source[None, :] == jnp.arange(ROWS)[:, None]).astype(BF16)
    leaving, attended, own = call(
        main_kernel,
        [(SHARDS * PACK, HALF), (TOK, HDT), (TOK, D)],
        (
            sharpness_coefficient,
            arrived,
            perm,
            back,
            weights,
            upstream_derivative[0],
            standardizer_multiplier.reshape(1, D),
            seen,
        ),
        [SM] + [VM] * 7,
        4 * 10**9,
        scratch=[
            pltpu.VMEM((ROWS, D), F32),
            pltpu.VMEM((ROWS, 128), F32),
            pltpu.VMEM((ROWS, D), BF16),
            pltpu.VMEM((ROWS, HDT), BF16),
            pltpu.VMEM((ROWS, HDT), BF16),
            pltpu.VMEM((ROWS, D), BF16),
            pltpu.VMEM((TOK, HDT), BF16),
            pltpu.VMEM((ROWS, D), F32),
        ],
        limit=48,
    )
    returned = lax.all_to_all(
        leaving.reshape(SHARDS, PACK, HALF), "tok", split_axis=0, concat_axis=0, tiled=True
    ).reshape(SHARDS * PACK, HALF)
    (layer_out,) = call(
        output_kernel,
        [(TOK, D)],
        (attended, own, weights),
        [VM] * 3,
        2 * TOK * HDT * D,
    )
    keep, send = call(
        collect_kernel,
        [(TOK, HALF)] * 2,
        (side, target, returned),
        [SM, VM, VM],
        2 * SHARDS * PACK * 2 * TOK * HALF,
    )
    recv = lax.ppermute(send, "tok", partner)
    (grad_tokens,) = call(
        restore_kernel,
        [(TOK, D)],
        (side, order, keep, recv),
        [SM, VM, VM, VM],
        2 * TOK * TOK * D,
    )
    return (layer_out[None], grad_tokens[None])


def solution(mesh):
    placed = (
        P("fsdp", "tok", None),
        P("fsdp", "tok", None),
        P("fsdp", None),
        P("fsdp", None, None),
        P("fsdp", None),
        P(),
        P(),
        P("fsdp", None),
        P("fsdp", None),
        P("fsdp", None),
        P(None, "fsdp"),
        P("fsdp", "tok", None),
    )
    return jax.shard_map(
        body,
        mesh=mesh,
        in_specs=placed,
        out_specs=(P("fsdp", "tok", None), P("fsdp", "tok", None)),
        check_vma=False,
    )
```

```python
import jax
import jax.numpy as jnp
from jax import lax
from jax.experimental import pallas as pl
from jax.experimental.pallas import tpu as pltpu
from jax.sharding import PartitionSpec as P

HEADS = 8
HEAD_DIM = 64
BLOCK = 64
HB = BLOCK // 2
KN = 4
D = 1024
HDT = 512
SHARDS = 32
TOK = 128
NB = 2
CHUNK = 4
SLOTS = 1 + KN
ITEMS = NB * SLOTS
ROWS = ITEMS * BLOCK
KEYS = SLOTS * BLOCK
HALF = D // 2
FAR = ROWS + ROWS // 2
PACK = ITEMS * CHUNK
GROUP = 4
GL = GROUP * HEAD_DIM
GR = GROUP * BLOCK

CHIPS = 8
SHARE = 64
STEPS = (0, 1, -1, 2, -2, 3, -3, 4)

norm_eps = 1e-05
head_eps = 1e-06
F32 = jnp.float32
BF16 = jnp.bfloat16
VM = pl.BlockSpec(memory_space=pltpu.VMEM)
SM = pl.BlockSpec(memory_space=pltpu.SMEM)
NN = (((1,), (0,)), ((), ()))
NT = (((1,), (1,)), ((), ()))
TN = (((0,), (0,)), ((), ()))


def dot(a, b, dims, **kw):
    return lax.dot_general(a, b, dims, preferred_element_type=F32, **kw)


def rolled(m):
    return jnp.concatenate([m[:BLOCK], m[BLOCK + HB :], m[BLOCK : BLOCK + HB]], axis=0)


def one_hot(row_ref, rows):
    idx = row_ref[...]
    iota = lax.broadcasted_iota(jnp.int32, (rows, idx.shape[1]), 0)
    return jnp.where(iota == idx, 1.0, 0.0).astype(BF16)


def arrange_kernel(
    side_ref, order_ref, x_ref, wq_ref, wk_ref, wv_ref, wo_ref, keep_ref, send_ref, share_ref
):
    for n, part in enumerate((wq_ref, wk_ref, wv_ref, wo_ref)):
        share_ref[:, n * HDT : (n + 1) * HDT] = part[...]
    a = dot(one_hot(order_ref, TOK), x_ref[...], TN).astype(BF16)
    lower = side_ref[0] == 0
    left, right = a[:, :HALF], a[:, HALF:]
    keep_ref[...] = jnp.where(lower, left, right)
    send_ref[...] = jnp.where(lower, right, left)


def stack_kernel(place_ref, *refs):
    out_ref = refs[-1]
    for step, ref in zip(STEPS, refs[:-1]):
        place = lax.rem(place_ref[0] + (CHIPS - step), CHIPS)
        out_ref[pl.ds(place * SHARE, SHARE), :] = ref[...]


def merge_kernel(place_ref, mine_ref, other_ref, out_ref):
    first = place_ref[1] == 0
    for y in range(CHIPS):
        rows = slice(y * SHARE, (y + 1) * SHARE)
        mine, other = mine_ref[rows, :], other_ref[rows, :]
        out_ref[2 * y * SHARE : (2 * y + 1) * SHARE, :] = jnp.where(first, mine, other)
        out_ref[(2 * y + 1) * SHARE : (2 * y + 2) * SHARE, :] = jnp.where(first, other, mine)


def pack_kernel(side_ref, target_ref, keep_ref, recv_ref, out_ref):
    lower = side_ref[0] == 0
    keep, recv = keep_ref[...], recv_ref[...]
    table = jnp.concatenate(
        [jnp.where(lower, keep, recv), jnp.where(lower, recv, keep)], axis=0
    )
    out_ref[...] = dot(one_hot(target_ref, 2 * TOK), table, TN).astype(BF16)


def collect_kernel(side_ref, target_ref, in_ref, keep_ref, send_ref):
    total = dot(one_hot(target_ref, 2 * TOK), in_ref[...], NN).astype(BF16)
    lower = side_ref[0] == 0
    even, odd = total[:TOK], total[TOK:]
    keep_ref[...] = jnp.where(lower, even, odd)
    send_ref[...] = jnp.where(lower, odd, even)


def restore_kernel(side_ref, order_ref, keep_ref, recv_ref, out_ref):
    lower = side_ref[0] == 0
    keep, recv = keep_ref[...], recv_ref[...]
    both = jnp.concatenate(
        [jnp.where(lower, keep, recv), jnp.where(lower, recv, keep)], axis=1
    )
    out_ref[...] = dot(one_hot(order_ref, TOK), both, NN).astype(BF16)


def main_kernel(
    sharp_ref,
    in_ref,
    perm_ref,
    back_ref,
    w_ref,
    up_ref,
    gain_ref,
    seen_ref,
    out_ref,
    att_ref,
    own_ref,
    normed_ref,
    rstd_ref,
    xn_ref,
    k_ref,
    v_ref,
    gkv_ref,
    gq_ref,
    gh_ref,
):
    x_in = jnp.concatenate(
        [in_ref[:ROWS], jnp.concatenate([in_ref[FAR:], in_ref[ROWS:FAR]], axis=0)], axis=1
    )
    normed_ref[...] = dot(perm_ref[...], x_in, NN)
    gain = gain_ref[...].astype(F32)
    for t in range(ITEMS):
        rows = pl.ds(t * BLOCK, BLOCK)
        x = normed_ref[rows, :]
        if t % SLOTS == 0:
            own_ref[pl.ds(t // SLOTS * BLOCK, BLOCK), :] = x.astype(BF16)
        centered = x - jnp.mean(x, axis=1, keepdims=True)
        rstd = 1.0 / jnp.sqrt(jnp.mean(centered * centered, axis=1, keepdims=True) + norm_eps)
        normed = centered * rstd
        normed_ref[rows, :] = normed
        rstd_ref[rows, :] = jnp.broadcast_to(rstd, (BLOCK, 128))
        xn_ref[rows, :] = (normed * gain).astype(BF16)
    xn = xn_ref[...]
    k_ref[...] = dot(xn, w_ref[:, HDT : 2 * HDT], NN).astype(BF16)
    v_ref[...] = dot(xn, w_ref[:, 2 * HDT : 3 * HDT], NN).astype(BF16)
    xn_own = jnp.concatenate([xn_ref[pl.ds(b * KEYS, BLOCK), :] for b in range(NB)], axis=0)
    queries = dot(xn_own, w_ref[:, :HDT], NN).astype(BF16)
    up = rolled(up_ref[...])
    grad_attn = dot(up, w_ref[:, 3 * HDT :], NN).astype(BF16)

    lane_head = lax.broadcasted_iota(jnp.int32, (BLOCK, GL), 1) // HEAD_DIM
    head_pick = (
        lax.broadcasted_iota(jnp.int32, (HEADS, HDT), 1) // HEAD_DIM
        == lax.broadcasted_iota(jnp.int32, (HEADS, HDT), 0)
    ).astype(F32)
    group_pick = (
        lax.broadcasted_iota(jnp.int32, (8, GL), 1) // HEAD_DIM
        == lax.broadcasted_iota(jnp.int32, (8, GL), 0)
    ).astype(F32)
    diagonal = lax.broadcasted_iota(jnp.int32, (BLOCK, KEYS), 0) == lax.broadcasted_iota(
        jnp.int32, (BLOCK, KEYS), 1
    )

    def spread(m):
        return jnp.concatenate(
            [jnp.where(lane_head == h, m, jnp.zeros_like(m)) for h in range(GROUP)], axis=0
        )

    def gather_heads(m):
        total = jnp.where(lane_head == 0, m[:BLOCK], 0.0)
        for h in range(1, GROUP):
            total = jnp.where(lane_head == h, m[h * BLOCK : (h + 1) * BLOCK], total)
        return total

    for b in range(NB):
        keys = pl.ds(b * KEYS, KEYS)
        own = slice(b * BLOCK, (b + 1) * BLOCK)
        kf = k_ref[keys, :].astype(F32)
        norm2 = dot(head_pick, kf * kf, NT, precision=lax.Precision.HIGHEST)
        inv_k = 1.0 / jnp.sqrt(norm2 + head_eps)
        allowed = (seen_ref[b : b + 1, :] > 0.0) | diagonal
        mask = jnp.concatenate([allowed] * GROUP, axis=0)
        for g in range(HEADS // GROUP):
            lanes = slice(g * GL, (g + 1) * GL)
            qm = spread(queries[own, lanes])
            gm = spread(grad_attn[own, lanes])
            k4 = k_ref[keys, lanes]
            v4 = v_ref[keys, lanes]
            qf = qm.astype(F32)
            inv_q = 1.0 / jnp.sqrt(jnp.sum(qf * qf, axis=1, keepdims=True) + head_eps)
            sharp = jnp.concatenate(
                [jnp.full((BLOCK, 1), sharp_ref[g * GROUP + h], F32) for h in range(GROUP)], axis=0
            )
            ik = inv_k[g * GROUP : (g + 1) * GROUP]
            ik_rows = jnp.concatenate(
                [jnp.broadcast_to(ik[h : h + 1], (BLOCK, KEYS)) for h in range(GROUP)], axis=0
            )
            factor = (sharp * inv_q) * ik_rows
            scores = factor * dot(qm, k4, NT)
            expo = jnp.where(mask, jnp.exp(scores), 0.0)
            prob = expo * (1.0 / jnp.sum(expo, axis=1, keepdims=True))
            prob_b = prob.astype(BF16)
            att_ref[own, lanes] = gather_heads(dot(prob_b, v4, NN)).astype(BF16)
            dprob = dot(gm, v4, NT)
            delta = jnp.sum(prob * dprob, axis=1, keepdims=True)
            dscore = prob * (dprob - delta)
            weighted = (factor * dscore).astype(BF16)
            score_grad = scores * dscore
            row_terms = jnp.sum(score_grad, axis=1, keepdims=True)
            gq = dot(weighted, k4, NN) - (inv_q * inv_q * row_terms) * qf
            gq_ref[own, lanes] = gather_heads(gq).astype(BF16)
            col_terms = jnp.concatenate(
                [
                    jnp.sum(score_grad[h * BLOCK : (h + 1) * BLOCK], axis=0, keepdims=True)
                    for h in range(GROUP)
                ],
                axis=0,
            )
            coef = ik * ik * col_terms
            coef = jnp.concatenate([coef, jnp.zeros_like(coef)], axis=0)
            coef = dot(coef, group_pick, TN, precision=lax.Precision.HIGHEST)
            gk = dot(weighted, qm, TN) - coef * k4.astype(F32)
            gkv_ref[keys, g * GL : (g + 1) * GL] = gk.astype(BF16)
            gkv_ref[keys, HDT + g * GL : HDT + (g + 1) * GL] = dot(prob_b, gm, TN).astype(BF16)

    gh_ref[...] = dot(gkv_ref[...], w_ref[:, HDT : 3 * HDT], NT)
    gq_hidden = dot(gq_ref[...], w_ref[:, :HDT], NT)
    for t in range(ITEMS):
        rows = pl.ds(t * BLOCK, BLOCK)
        hidden = gh_ref[rows, :]
        b = t // SLOTS
        if t % SLOTS == 0:
            hidden = hidden + gq_hidden[b * BLOCK : (b + 1) * BLOCK]
        grad = hidden * gain
        normed = normed_ref[rows, :]
        m1 = jnp.mean(grad, axis=1, keepdims=True)
        m2 = jnp.mean(grad * normed, axis=1, keepdims=True)
        grad = rstd_ref[rows, 0:1] * (grad - m1 - normed * m2)
        if t % SLOTS == 0:
            grad = grad + up[b * BLOCK : (b + 1) * BLOCK].astype(F32)
        xn_ref[rows, :] = grad.astype(BF16)
    back = dot(back_ref[...], xn_ref[...], NN).astype(BF16)
    out_ref[:ROWS] = back[:, :HALF]
    out_ref[FAR:] = back[: ROWS // 2, HALF:]
    out_ref[ROWS:FAR] = back[ROWS // 2 :, HALF:]


def output_kernel(att_ref, own_ref, w_ref, out_ref):
    out = own_ref[...].astype(F32) + dot(att_ref[...], w_ref[:, 3 * HDT :], NT)
    out_ref[...] = rolled(out.astype(BF16))


def call(kernel, outs, args, specs, flops, scratch=(), limit=16):
    outs = [jax.ShapeDtypeStruct(shape, BF16) for shape in outs]
    moved = sum(a.size * a.dtype.itemsize for a in list(args) + outs)
    return pl.pallas_call(
        kernel,
        out_shape=outs,
        in_specs=specs,
        out_specs=[VM] * len(outs),
        scratch_shapes=list(scratch),
        compiler_params=pltpu.CompilerParams(vmem_limit_bytes=limit * 2**20),
        cost_estimate=pl.CostEstimate(flops=flops, bytes_accessed=moved, transcendentals=0),
    )(*args)


def gather_weights(share, place):
    members = 2 * CHIPS
    upward = [(i, (i + 2) % members) for i in range(members)]
    downward = [(i, (i - 2) % members) for i in range(members)]
    pieces, up, down = [share], share, share
    for _ in range(CHIPS // 2 - 1):
        up = lax.ppermute(up, "fsdp", upward)
        down = lax.ppermute(down, "fsdp", downward)
        pieces += [up, down]
    pieces.append(lax.ppermute(up, "fsdp", upward))
    (mine,) = call(
        stack_kernel, [(CHIPS * SHARE, 4 * HDT)], (place, *pieces), [SM] + [VM] * CHIPS, 0
    )
    other = lax.ppermute(mine, "fsdp", [(i, i ^ 1) for i in range(members)])
    (weights,) = call(merge_kernel, [(D, 4 * HDT)], (place, mine, other), [SM, VM, VM], 0)
    return weights


def body(
    embedded_pieces,
    morton_arrangement,
    unhidden_indicator,
    bordering_tiles,
    bordering_tally,
    standardizer_multiplier,
    sharpness_coefficient,
    probe_projector,
    lookup_projector,
    content_projector,
    result_projector,
    upstream_derivative,
):
    me = lax.axis_index("tok")
    side = (me // (SHARDS // 2)).reshape(1).astype(jnp.int32)
    column = SHARDS // 4
    partner = [(i, (3 - i // column) * column + i % column) for i in range(SHARDS)]
    member = lax.axis_index("fsdp").astype(jnp.int32)
    place = jnp.stack([member // 2, member % 2])

    order = morton_arrangement[0]
    keep, send, share = call(
        arrange_kernel,
        [(TOK, HALF)] * 2 + [(SHARE, 4 * HDT)],
        (
            side,
            order,
            embedded_pieces[0],
            probe_projector,
            lookup_projector,
            content_projector,
            result_projector.T,
        ),
        [SM] + [VM] * 6,
        2 * TOK * TOK * D,
    )
    recv = lax.ppermute(send, "tok", partner)
    weights = gather_weights(share, place)

    lists = bordering_tiles[0].reshape(SHARDS, NB, KN)
    own_blocks = jnp.arange(SHARDS * NB, dtype=jnp.int32).reshape(SHARDS, NB, 1)
    named = jnp.concatenate([own_blocks, lists], axis=2).reshape(SHARDS, ITEMS)
    target = (named % 2) * TOK + (named // 2) * CHUNK
    target = (target[:, :, None] + jnp.arange(CHUNK, dtype=jnp.int32)).reshape(
        1, SHARDS * PACK
    )
    (packed,) = call(
        pack_kernel,
        [(SHARDS * PACK, HALF)],
        (side, target, keep, recv),
        [SM, VM, VM, VM],
        2 * SHARDS * PACK * 2 * TOK * HALF,
    )
    arrived = lax.all_to_all(
        packed.reshape(SHARDS, PACK, HALF), "tok", split_axis=0, concat_axis=0, tiled=True
    ).reshape(SHARDS * PACK, HALF)

    seen_all = unhidden_indicator[0].reshape(SHARDS, NB, BLOCK).astype(F32)
    seen_all = jnp.stack(
        [
            seen_all[:, 0],
            jnp.concatenate([seen_all[:, 1, HB:], seen_all[:, 1, :HB]], axis=1),
        ],
        axis=1,
    ).reshape(SHARDS * NB, BLOCK)
    used = jnp.arange(SLOTS)[None, :] <= bordering_tally[0][:, None]
    used = used.reshape(SHARDS, ITEMS)
    picks = (
        (named[:, :, None] == jnp.arange(SHARDS * NB)) & used[:, :, None]
    ).astype(F32)
    picks = jnp.sum(picks * (jnp.arange(SHARDS) == me)[:, None, None], axis=0)
    seen = jnp.dot(picks, seen_all).reshape(NB, KEYS)

    dest = jnp.arange(ROWS)
    source = (dest % BLOCK // CHUNK) * PACK + (dest // BLOCK) * CHUNK + dest % CHUNK
    perm = (source[:, None] == jnp.arange(ROWS)[None, :]).astype(BF16)
    back = (source[None, :] == jnp.arange(ROWS)[:, None]).astype(BF16)
    leaving, attended, own = call(
        main_kernel,
        [(SHARDS * PACK, HALF), (TOK, HDT), (TOK, D)],
        (
            sharpness_coefficient,
            arrived,
            perm,
            back,
            weights,
            upstream_derivative[0],
            standardizer_multiplier.reshape(1, D),
            seen,
        ),
        [SM] + [VM] * 7,
        4 * 10**9,
        scratch=[
            pltpu.VMEM((ROWS, D), F32),
            pltpu.VMEM((ROWS, 128), F32),
            pltpu.VMEM((ROWS, D), BF16),
            pltpu.VMEM((ROWS, HDT), BF16),
            pltpu.VMEM((ROWS, HDT), BF16),
            pltpu.VMEM((ROWS, D), BF16),
            pltpu.VMEM((TOK, HDT), BF16),
            pltpu.VMEM((ROWS, D), F32),
        ],
        limit=48,
    )
    returned = lax.all_to_all(
        leaving.reshape(SHARDS, PACK, HALF), "tok", split_axis=0, concat_axis=0, tiled=True
    ).reshape(SHARDS * PACK, HALF)
    (layer_out,) = call(
        output_kernel,
        [(TOK, D)],
        (attended, own, weights),
        [VM] * 3,
        2 * TOK * HDT * D,
    )
    keep, send = call(
        collect_kernel,
        [(TOK, HALF)] * 2,
        (side, target, returned),
        [SM, VM, VM],
        2 * SHARDS * PACK * 2 * TOK * HALF,
    )
    recv = lax.ppermute(send, "tok", partner)
    (grad_tokens,) = call(
        restore_kernel,
        [(TOK, D)],
        (side, order, keep, recv),
        [SM, VM, VM, VM],
        2 * TOK * TOK * D,
    )
    return (layer_out[None], grad_tokens[None])


def solution(mesh):
    placed = (
        P("fsdp", "tok", None),
        P("fsdp", "tok", None),
        P("fsdp", None),
        P("fsdp", None, None),
        P("fsdp", None),
        P(),
        P(),
        P("fsdp", None),
        P("fsdp", None),
        P("fsdp", None),
        P(None, "fsdp"),
        P("fsdp", "tok", None),
    )
    return jax.shard_map(
        body,
        mesh=mesh,
        in_specs=placed,
        out_specs=(P("fsdp", "tok", None), P("fsdp", "tok", None)),
        check_vma=False,
    )
```

```python
import jax
import jax.numpy as jnp
from jax import lax
from jax.experimental import pallas as pl
from jax.experimental.pallas import tpu as pltpu
from jax.sharding import PartitionSpec as P

HEADS = 8
HEAD_DIM = 64
BLOCK = 64
HB = BLOCK // 2
KN = 4
D = 1024
HDT = 512
SHARDS = 32
TOK = 128
NB = 2
CHUNK = 4
SLOTS = 1 + KN
ITEMS = NB * SLOTS
ROWS = ITEMS * BLOCK
KEYS = SLOTS * BLOCK
HALF = D // 2
FAR = ROWS + ROWS // 2
PACK = ITEMS * CHUNK
GROUP = 4
GL = GROUP * HEAD_DIM
GR = GROUP * BLOCK

SHARE = 64

norm_eps = 1e-05
head_eps = 1e-06
F32 = jnp.float32
BF16 = jnp.bfloat16
VM = pl.BlockSpec(memory_space=pltpu.VMEM)
SM = pl.BlockSpec(memory_space=pltpu.SMEM)
HB_SPEC = pl.BlockSpec(memory_space=pltpu.HBM)
NN = (((1,), (0,)), ((), ()))
NT = (((1,), (1,)), ((), ()))
TN = (((0,), (0,)), ((), ()))


def dot(a, b, dims, **kw):
    return lax.dot_general(a, b, dims, preferred_element_type=F32, **kw)


def rolled(m):
    return jnp.concatenate([m[:BLOCK], m[BLOCK + HB :], m[BLOCK : BLOCK + HB]], axis=0)


def one_hot(row_ref, rows):
    idx = row_ref[...]
    iota = lax.broadcasted_iota(jnp.int32, (rows, idx.shape[1]), 0)
    return jnp.where(iota == idx, 1.0, 0.0).astype(BF16)


def arrange_kernel(
    side_ref,
    order_hbm,
    x_hbm,
    wq_hbm,
    wk_hbm,
    wv_hbm,
    wo_hbm,
    keep_ref,
    send_ref,
    share_ref,
    order_ref,
    x_ref,
    sems,
):
    copies = [
        pltpu.make_async_copy(x_hbm, x_ref, sems.at[0]),
        pltpu.make_async_copy(order_hbm, order_ref, sems.at[1]),
    ]
    for n, part in enumerate((wq_hbm, wk_hbm, wv_hbm, wo_hbm)):
        lanes = pl.ds(n * HDT, HDT)
        copies.append(pltpu.make_async_copy(part, share_ref.at[:, lanes], sems.at[2 + n]))
    for copy in copies:
        copy.start()
    for copy in copies:
        copy.wait()
    a = dot(one_hot(order_ref, TOK), x_ref[...], TN).astype(BF16)
    lower = side_ref[0] == 0
    left, right = a[:, :HALF], a[:, HALF:]
    keep_ref[...] = jnp.where(lower, left, right)
    send_ref[...] = jnp.where(lower, right, left)


def pack_kernel(side_ref, target_ref, keep_ref, recv_ref, out_ref):
    lower = side_ref[0] == 0
    keep, recv = keep_ref[...], recv_ref[...]
    table = jnp.concatenate(
        [jnp.where(lower, keep, recv), jnp.where(lower, recv, keep)], axis=0
    )
    out_ref[...] = dot(one_hot(target_ref, 2 * TOK), table, TN).astype(BF16)


def collect_kernel(side_ref, target_ref, in_ref, keep_ref, send_ref):
    total = dot(one_hot(target_ref, 2 * TOK), in_ref[...], NN).astype(BF16)
    lower = side_ref[0] == 0
    even, odd = total[:TOK], total[TOK:]
    keep_ref[...] = jnp.where(lower, even, odd)
    send_ref[...] = jnp.where(lower, odd, even)


def restore_kernel(side_ref, order_ref, keep_ref, recv_ref, out_ref):
    lower = side_ref[0] == 0
    keep, recv = keep_ref[...], recv_ref[...]
    both = jnp.concatenate(
        [jnp.where(lower, keep, recv), jnp.where(lower, recv, keep)], axis=1
    )
    out_ref[...] = dot(one_hot(order_ref, TOK), both, NN).astype(BF16)


def source(dest):
    return (dest % BLOCK // CHUNK) * PACK + (dest // BLOCK) * CHUNK + dest % CHUNK


def main_kernel(
    sharp_ref,
    in_ref,
    w_hbm,
    up_hbm,
    gain_ref,
    seen_ref,
    out_ref,
    att_ref,
    own_ref,
    wo_ref,
    w_ref,
    up_ref,
    sems,
    normed_ref,
    rstd_ref,
    xn_ref,
    back_ref,
    k_ref,
    v_ref,
    gkv_ref,
    gq_ref,
    gh_ref,
):
    copies = [
        pltpu.make_async_copy(w_hbm.at[:, pl.ds(0, 3 * HDT)], w_ref, sems.at[0]),
        pltpu.make_async_copy(w_hbm.at[:, pl.ds(3 * HDT, HDT)], wo_ref, sems.at[1]),
        pltpu.make_async_copy(up_hbm, up_ref, sems.at[2]),
    ]
    for copy in copies:
        copy.start()
    shape = (ROWS, ROWS)
    row = source(lax.broadcasted_iota(jnp.int32, (ROWS, 1), 0))
    perm = row == lax.broadcasted_iota(jnp.int32, shape, 1)
    column = source(lax.broadcasted_iota(jnp.int32, (1, ROWS), 1))
    back = column == lax.broadcasted_iota(jnp.int32, shape, 0)
    back_ref[...] = jnp.where(back, 1.0, 0.0).astype(BF16)
    x_in = jnp.concatenate(
        [in_ref[:ROWS], jnp.concatenate([in_ref[FAR:], in_ref[ROWS:FAR]], axis=0)], axis=1
    )
    normed_ref[...] = dot(jnp.where(perm, 1.0, 0.0).astype(BF16), x_in, NN)
    gain = gain_ref[...].astype(F32)
    for t in range(ITEMS):
        rows = pl.ds(t * BLOCK, BLOCK)
        x = normed_ref[rows, :]
        if t % SLOTS == 0:
            own_ref[pl.ds(t // SLOTS * BLOCK, BLOCK), :] = x.astype(BF16)
        centered = x - jnp.mean(x, axis=1, keepdims=True)
        rstd = 1.0 / jnp.sqrt(jnp.mean(centered * centered, axis=1, keepdims=True) + norm_eps)
        normed = centered * rstd
        normed_ref[rows, :] = normed
        rstd_ref[rows, :] = jnp.broadcast_to(rstd, (BLOCK, 128))
        xn_ref[rows, :] = (normed * gain).astype(BF16)
    for copy in copies:
        copy.wait()
    xn = xn_ref[...]
    k_ref[...] = dot(xn, w_ref[:, HDT : 2 * HDT], NN).astype(BF16)
    v_ref[...] = dot(xn, w_ref[:, 2 * HDT : 3 * HDT], NN).astype(BF16)
    xn_own = jnp.concatenate([xn_ref[pl.ds(b * KEYS, BLOCK), :] for b in range(NB)], axis=0)
    queries = dot(xn_own, w_ref[:, :HDT], NN).astype(BF16)
    up = rolled(up_ref[...])
    grad_attn = dot(up, wo_ref[...], NN).astype(BF16)

    lane_head = lax.broadcasted_iota(jnp.int32, (BLOCK, GL), 1) // HEAD_DIM
    head_pick = (
        lax.broadcasted_iota(jnp.int32, (HEADS, HDT), 1) // HEAD_DIM
        == lax.broadcasted_iota(jnp.int32, (HEADS, HDT), 0)
    ).astype(F32)
    group_pick = (
        lax.broadcasted_iota(jnp.int32, (8, GL), 1) // HEAD_DIM
        == lax.broadcasted_iota(jnp.int32, (8, GL), 0)
    ).astype(F32)
    diagonal = lax.broadcasted_iota(jnp.int32, (BLOCK, KEYS), 0) == lax.broadcasted_iota(
        jnp.int32, (BLOCK, KEYS), 1
    )

    def spread(m):
        return jnp.concatenate(
            [jnp.where(lane_head == h, m, jnp.zeros_like(m)) for h in range(GROUP)], axis=0
        )

    def gather_heads(m):
        total = jnp.where(lane_head == 0, m[:BLOCK], 0.0)
        for h in range(1, GROUP):
            total = jnp.where(lane_head == h, m[h * BLOCK : (h + 1) * BLOCK], total)
        return total

    for b in range(NB):
        keys = pl.ds(b * KEYS, KEYS)
        own = slice(b * BLOCK, (b + 1) * BLOCK)
        kf = k_ref[keys, :].astype(F32)
        norm2 = dot(head_pick, kf * kf, NT, precision=lax.Precision.HIGHEST)
        inv_k = 1.0 / jnp.sqrt(norm2 + head_eps)
        allowed = (seen_ref[b : b + 1, :] > 0.0) | diagonal
        mask = jnp.concatenate([allowed] * GROUP, axis=0)
        for g in range(HEADS // GROUP):
            lanes = slice(g * GL, (g + 1) * GL)
            qm = spread(queries[own, lanes])
            gm = spread(grad_attn[own, lanes])
            k4 = k_ref[keys, lanes]
            v4 = v_ref[keys, lanes]
            qf = qm.astype(F32)
            inv_q = 1.0 / jnp.sqrt(jnp.sum(qf * qf, axis=1, keepdims=True) + head_eps)
            sharp = jnp.concatenate(
                [jnp.full((BLOCK, 1), sharp_ref[g * GROUP + h], F32) for h in range(GROUP)], axis=0
            )
            ik = inv_k[g * GROUP : (g + 1) * GROUP]
            ik_rows = jnp.concatenate(
                [jnp.broadcast_to(ik[h : h + 1], (BLOCK, KEYS)) for h in range(GROUP)], axis=0
            )
            factor = (sharp * inv_q) * ik_rows
            scores = factor * dot(qm, k4, NT)
            expo = jnp.where(mask, jnp.exp(scores), 0.0)
            prob = expo * (1.0 / jnp.sum(expo, axis=1, keepdims=True))
            prob_b = prob.astype(BF16)
            att_ref[own, lanes] = gather_heads(dot(prob_b, v4, NN)).astype(BF16)
            dprob = dot(gm, v4, NT)
            delta = jnp.sum(prob * dprob, axis=1, keepdims=True)
            dscore = prob * (dprob - delta)
            weighted = (factor * dscore).astype(BF16)
            score_grad = scores * dscore
            row_terms = jnp.sum(score_grad, axis=1, keepdims=True)
            gq = dot(weighted, k4, NN) - (inv_q * inv_q * row_terms) * qf
            gq_ref[own, lanes] = gather_heads(gq).astype(BF16)
            col_terms = jnp.concatenate(
                [
                    jnp.sum(score_grad[h * BLOCK : (h + 1) * BLOCK], axis=0, keepdims=True)
                    for h in range(GROUP)
                ],
                axis=0,
            )
            coef = ik * ik * col_terms
            coef = jnp.concatenate([coef, jnp.zeros_like(coef)], axis=0)
            coef = dot(coef, group_pick, TN, precision=lax.Precision.HIGHEST)
            gk = dot(weighted, qm, TN) - coef * k4.astype(F32)
            gkv_ref[keys, g * GL : (g + 1) * GL] = gk.astype(BF16)
            gkv_ref[keys, HDT + g * GL : HDT + (g + 1) * GL] = dot(prob_b, gm, TN).astype(BF16)

    gh_ref[...] = dot(gkv_ref[...], w_ref[:, HDT : 3 * HDT], NT)
    gq_hidden = dot(gq_ref[...], w_ref[:, :HDT], NT)
    for t in range(ITEMS):
        rows = pl.ds(t * BLOCK, BLOCK)
        hidden = gh_ref[rows, :]
        b = t // SLOTS
        if t % SLOTS == 0:
            hidden = hidden + gq_hidden[b * BLOCK : (b + 1) * BLOCK]
        grad = hidden * gain
        normed = normed_ref[rows, :]
        m1 = jnp.mean(grad, axis=1, keepdims=True)
        m2 = jnp.mean(grad * normed, axis=1, keepdims=True)
        grad = rstd_ref[rows, 0:1] * (grad - m1 - normed * m2)
        if t % SLOTS == 0:
            grad = grad + up[b * BLOCK : (b + 1) * BLOCK].astype(F32)
        xn_ref[rows, :] = grad.astype(BF16)
    back = dot(back_ref[...], xn_ref[...], NN).astype(BF16)
    out_ref[:ROWS] = back[:, :HALF]
    out_ref[FAR:] = back[: ROWS // 2, HALF:]
    out_ref[ROWS:FAR] = back[ROWS // 2 :, HALF:]


def output_kernel(att_ref, own_ref, wo_ref, out_ref):
    out = own_ref[...].astype(F32) + dot(att_ref[...], wo_ref[...], NT)
    out_ref[...] = rolled(out.astype(BF16))


def call(kernel, outs, args, specs, flops, scratch=(), limit=8, out_spec=VM):
    place = pltpu.HBM if out_spec is HB_SPEC else jax.ShapeDtypeStruct
    moved = sum(a.size * a.dtype.itemsize for a in args)
    moved += sum(2 * o[0] * o[1] for o in outs)
    if flops == 0:
        moved = 0
    args = [
        pltpu.with_memory_space_constraint(a, pltpu.HBM) if spec is HB_SPEC else a
        for a, spec in zip(args, specs)
    ]
    return pl.pallas_call(
        kernel,
        out_shape=[place(o[:2], o[2] if len(o) > 2 else BF16) for o in outs],
        in_specs=specs,
        out_specs=[out_spec] * len(outs),
        scratch_shapes=list(scratch),
        compiler_params=pltpu.CompilerParams(vmem_limit_bytes=limit * 2**20),
        cost_estimate=pl.CostEstimate(flops=flops, bytes_accessed=moved, transcendentals=0),
    )(*args)


def body(
    embedded_pieces,
    morton_arrangement,
    unhidden_indicator,
    bordering_tiles,
    bordering_tally,
    standardizer_multiplier,
    sharpness_coefficient,
    probe_projector,
    lookup_projector,
    content_projector,
    result_projector,
    upstream_derivative,
):
    me = lax.axis_index("tok")
    side = (me // (SHARDS // 2)).reshape(1).astype(jnp.int32)
    column = SHARDS // 4
    partner = [(i, (3 - i // column) * column + i % column) for i in range(SHARDS)]

    order = morton_arrangement[0]
    keep, send, share = call(
        arrange_kernel,
        [(TOK, HALF)] * 2 + [(SHARE, 4 * HDT)],
        (
            side,
            order,
            embedded_pieces[0],
            probe_projector,
            lookup_projector,
            content_projector,
            result_projector.T,
        ),
        [SM] + [HB_SPEC] * 6,
        2 * TOK * TOK * D,
        scratch=[
            pltpu.VMEM((1, TOK), jnp.int32),
            pltpu.VMEM((TOK, D), BF16),
            pltpu.SemaphoreType.DMA((6,)),
        ],
    )
    weights = lax.all_gather(share, "fsdp", axis=0, tiled=True)
    recv = lax.ppermute(send, "tok", partner)

    lists = bordering_tiles[0].reshape(SHARDS, NB, KN)
    own_blocks = jnp.arange(SHARDS * NB, dtype=jnp.int32).reshape(SHARDS, NB, 1)
    named = jnp.concatenate([own_blocks, lists], axis=2).reshape(SHARDS, ITEMS)
    target = (named % 2) * TOK + (named // 2) * CHUNK
    target = (target[:, :, None] + jnp.arange(CHUNK, dtype=jnp.int32)).reshape(
        1, SHARDS * PACK
    )
    (packed,) = call(
        pack_kernel,
        [(SHARDS * PACK, HALF)],
        (side, target, keep, recv),
        [SM, VM, VM, VM],
        2 * SHARDS * PACK * 2 * TOK * HALF,
    )
    arrived = lax.all_to_all(
        packed.reshape(SHARDS, PACK, HALF), "tok", split_axis=0, concat_axis=0, tiled=True
    ).reshape(SHARDS * PACK, HALF)

    seen_all = unhidden_indicator[0].reshape(SHARDS, NB, BLOCK).astype(F32)
    seen_all = jnp.stack(
        [
            seen_all[:, 0],
            jnp.concatenate([seen_all[:, 1, HB:], seen_all[:, 1, :HB]], axis=1),
        ],
        axis=1,
    ).reshape(SHARDS * NB, BLOCK)
    used = jnp.arange(SLOTS)[None, :] <= bordering_tally[0][:, None]
    used = used.reshape(SHARDS, ITEMS)
    picks = (
        (named[:, :, None] == jnp.arange(SHARDS * NB)) & used[:, :, None]
    ).astype(F32)
    picks = jnp.sum(picks * (jnp.arange(SHARDS) == me)[:, None, None], axis=0)
    seen = jnp.dot(picks, seen_all).reshape(NB, KEYS)

    leaving, attended, own, out_weight = call(
        main_kernel,
        [(SHARDS * PACK, HALF), (TOK, HDT), (TOK, D), (D, HDT)],
        (
            sharpness_coefficient,
            arrived,
            weights,
            upstream_derivative[0],
            standardizer_multiplier.reshape(1, D),
            seen,
        ),
        [SM, VM, HB_SPEC, HB_SPEC, VM, VM],
        4 * 10**9,
        scratch=[
            pltpu.VMEM((D, 3 * HDT), BF16),
            pltpu.VMEM((TOK, D), BF16),
            pltpu.SemaphoreType.DMA((3,)),
            pltpu.VMEM((ROWS, D), F32),
            pltpu.VMEM((ROWS, 128), F32),
            pltpu.VMEM((ROWS, D), BF16),
            pltpu.VMEM((ROWS, ROWS), BF16),
            pltpu.VMEM((ROWS, HDT), BF16),
            pltpu.VMEM((ROWS, HDT), BF16),
            pltpu.VMEM((ROWS, D), BF16),
            pltpu.VMEM((TOK, HDT), BF16),
            pltpu.VMEM((ROWS, D), F32),
        ],
        limit=40,
    )
    returned = lax.all_to_all(
        leaving.reshape(SHARDS, PACK, HALF), "tok", split_axis=0, concat_axis=0, tiled=True
    ).reshape(SHARDS * PACK, HALF)
    (layer_out,) = call(
        output_kernel,
        [(TOK, D)],
        (attended, own, out_weight),
        [VM] * 3,
        2 * TOK * HDT * D,
    )
    keep, send = call(
        collect_kernel,
        [(TOK, HALF)] * 2,
        (side, target, returned),
        [SM, VM, VM],
        2 * SHARDS * PACK * 2 * TOK * HALF,
    )
    recv = lax.ppermute(send, "tok", partner)
    (grad_tokens,) = call(
        restore_kernel,
        [(TOK, D)],
        (side, order, keep, recv),
        [SM, VM, VM, VM],
        2 * TOK * TOK * D,
    )
    return (layer_out[None], grad_tokens[None])


def solution(mesh):
    placed = (
        P("fsdp", "tok", None),
        P("fsdp", "tok", None),
        P("fsdp", None),
        P("fsdp", None, None),
        P("fsdp", None),
        P(),
        P(),
        P("fsdp", None),
        P("fsdp", None),
        P("fsdp", None),
        P(None, "fsdp"),
        P("fsdp", "tok", None),
    )
    return jax.shard_map(
        body,
        mesh=mesh,
        in_specs=placed,
        out_specs=(P("fsdp", "tok", None), P("fsdp", "tok", None)),
        check_vma=False,
    )
```

```python
import jax
import jax.numpy as jnp
from jax import lax
from jax.experimental import pallas as pl
from jax.experimental.pallas import tpu as pltpu
from jax.sharding import PartitionSpec as P

HEADS = 8
HEAD_DIM = 64
BLOCK = 64
HB = BLOCK // 2
KN = 4
D = 1024
HDT = 512
SHARDS = 32
TOK = 128
NB = 2
CHUNK = 4
SLOTS = 1 + KN
ITEMS = NB * SLOTS
ROWS = ITEMS * BLOCK
KEYS = SLOTS * BLOCK
HALF = D // 2
QB = BLOCK // 4
QROWS = ROWS // 4
FAR = ROWS + ROWS // 2
PACK = ITEMS * CHUNK
GROUP = 4
GL = GROUP * HEAD_DIM
GR = GROUP * BLOCK

SHARE = 64

norm_eps = 1e-05
head_eps = 1e-06
F32 = jnp.float32
BF16 = jnp.bfloat16
VM = pl.BlockSpec(memory_space=pltpu.VMEM)
SM = pl.BlockSpec(memory_space=pltpu.SMEM)
HB_SPEC = pl.BlockSpec(memory_space=pltpu.HBM)
NN = (((1,), (0,)), ((), ()))
NT = (((1,), (1,)), ((), ()))
TN = (((0,), (0,)), ((), ()))


def dot(a, b, dims, **kw):
    return lax.dot_general(a, b, dims, preferred_element_type=F32, **kw)


def rolled(m):
    return jnp.concatenate([m[:BLOCK], m[BLOCK + HB :], m[BLOCK : BLOCK + HB]], axis=0)


def split_dot(a, b, dims, which):
    exact = a if which == 0 else b
    high = exact.astype(BF16)
    low = (exact - high.astype(F32)).astype(BF16)
    if which == 0:
        return dot(high, b, dims) + dot(low, b, dims)
    return dot(a, high, dims) + dot(a, low, dims)


def one_hot(row_ref, rows):
    idx = row_ref[...]
    iota = lax.broadcasted_iota(jnp.int32, (rows, idx.shape[1]), 0)
    return jnp.where(iota == idx, 1.0, 0.0).astype(BF16)


def arrange_kernel(
    side_ref,
    order_hbm,
    x_hbm,
    wq_hbm,
    wk_hbm,
    wv_hbm,
    wo_hbm,
    keep_ref,
    send_ref,
    share_ref,
    order_ref,
    x_ref,
    sems,
):
    copies = [
        pltpu.make_async_copy(x_hbm, x_ref, sems.at[0]),
        pltpu.make_async_copy(order_hbm, order_ref, sems.at[1]),
    ]
    for n, part in enumerate((wq_hbm, wk_hbm, wv_hbm, wo_hbm)):
        lanes = pl.ds(n * HDT, HDT)
        copies.append(pltpu.make_async_copy(part, share_ref.at[:, lanes], sems.at[2 + n]))
    for copy in copies:
        copy.start()
    for copy in copies:
        copy.wait()
    a = dot(one_hot(order_ref, TOK), x_ref[...], TN).astype(BF16)
    lower = side_ref[0] == 0
    left, right = a[:, :HALF], a[:, HALF:]
    keep_ref[...] = jnp.where(lower, left, right)
    send_ref[...] = jnp.where(lower, right, left)


def pack_kernel(side_ref, target_ref, keep_ref, recv_ref, out_ref):
    lower = side_ref[0] == 0
    keep, recv = keep_ref[...], recv_ref[...]
    table = jnp.concatenate(
        [jnp.where(lower, keep, recv), jnp.where(lower, recv, keep)], axis=0
    )
    out_ref[...] = dot(one_hot(target_ref, 2 * TOK), table, TN).astype(BF16)


def collect_kernel(side_ref, target_ref, in_ref, keep_ref, send_ref):
    total = dot(one_hot(target_ref, 2 * TOK), in_ref[...], NN).astype(BF16)
    lower = side_ref[0] == 0
    even, odd = total[:TOK], total[TOK:]
    keep_ref[...] = jnp.where(lower, even, odd)
    send_ref[...] = jnp.where(lower, odd, even)


def restore_kernel(side_ref, order_ref, keep_ref, recv_ref, out_ref):
    lower = side_ref[0] == 0
    keep, recv = keep_ref[...], recv_ref[...]
    both = jnp.concatenate(
        [jnp.where(lower, keep, recv), jnp.where(lower, recv, keep)], axis=1
    )
    out_ref[...] = dot(one_hot(order_ref, TOK), both, NN).astype(BF16)


def source(dest):
    return (dest % QB // CHUNK) * PACK + (dest // QB) * CHUNK + dest % CHUNK


def quarter(q):
    right = FAR + q * QROWS if q < 2 else ROWS + (q - 2) * QROWS
    return slice(q * QROWS, (q + 1) * QROWS), slice(right, right + QROWS)


def main_kernel(
    sharp_ref,
    in_ref,
    w_hbm,
    up_hbm,
    gain_ref,
    seen_ref,
    out_ref,
    att_ref,
    own_ref,
    wo_ref,
    w_ref,
    up_ref,
    sems,
    normed_ref,
    rstd_ref,
    xn_ref,
    k_ref,
    v_ref,
    gkv_ref,
    gq_ref,
    gh_ref,
):
    copies = [
        pltpu.make_async_copy(w_hbm.at[:, pl.ds(0, 3 * HDT)], w_ref, sems.at[0]),
        pltpu.make_async_copy(w_hbm.at[:, pl.ds(3 * HDT, HDT)], wo_ref, sems.at[1]),
        pltpu.make_async_copy(up_hbm, up_ref, sems.at[2]),
    ]
    for copy in copies:
        copy.start()
    shape = (QROWS, QROWS)
    row = source(lax.broadcasted_iota(jnp.int32, (QROWS, 1), 0))
    perm = jnp.where(row == lax.broadcasted_iota(jnp.int32, shape, 1), 1.0, 0.0).astype(BF16)
    column = source(lax.broadcasted_iota(jnp.int32, (1, QROWS), 1))
    back = jnp.where(column == lax.broadcasted_iota(jnp.int32, shape, 0), 1.0, 0.0).astype(BF16)
    for q in range(4):
        left, right = quarter(q)
        x_in = jnp.concatenate([in_ref[left, :], in_ref[right, :]], axis=1)
        x = dot(perm, x_in, NN)
        for t in range(ITEMS):
            at = t * BLOCK + q * QB
            normed_ref[at : at + QB, :] = x[t * QB : (t + 1) * QB]
    gain = gain_ref[...].astype(F32)
    for t in range(ITEMS):
        rows = pl.ds(t * BLOCK, BLOCK)
        x = normed_ref[rows, :]
        if t % SLOTS == 0:
            own_ref[pl.ds(t // SLOTS * BLOCK, BLOCK), :] = x.astype(BF16)
        centered = x - jnp.mean(x, axis=1, keepdims=True)
        rstd = 1.0 / jnp.sqrt(jnp.mean(centered * centered, axis=1, keepdims=True) + norm_eps)
        normed = centered * rstd
        normed_ref[rows, :] = normed
        rstd_ref[rows, :] = jnp.broadcast_to(rstd, (BLOCK, 128))
        xn_ref[rows, :] = (normed * gain).astype(BF16)
    for copy in copies:
        copy.wait()
    xn = xn_ref[...]
    k_ref[...] = dot(xn, w_ref[:, HDT : 2 * HDT], NN).astype(BF16)
    v_ref[...] = dot(xn, w_ref[:, 2 * HDT : 3 * HDT], NN).astype(BF16)
    xn_own = jnp.concatenate([xn_ref[pl.ds(b * KEYS, BLOCK), :] for b in range(NB)], axis=0)
    queries = dot(xn_own, w_ref[:, :HDT], NN).astype(BF16)
    up = rolled(up_ref[...])
    grad_attn = dot(up, wo_ref[...], NN).astype(BF16)

    lane_head = lax.broadcasted_iota(jnp.int32, (BLOCK, GL), 1) // HEAD_DIM
    def picks(shape):
        hit = lax.broadcasted_iota(jnp.int32, shape, 1) // HEAD_DIM == lax.broadcasted_iota(
            jnp.int32, shape, 0
        )
        return jnp.where(hit, 1.0, 0.0).astype(BF16)

    head_pick = picks((16, HDT))
    group_pick = picks((16, GL))
    diagonal = lax.broadcasted_iota(jnp.int32, (BLOCK, KEYS), 0) == lax.broadcasted_iota(
        jnp.int32, (BLOCK, KEYS), 1
    )

    def spread(m):
        return jnp.concatenate(
            [jnp.where(lane_head == h, m, jnp.zeros_like(m)) for h in range(GROUP)], axis=0
        )

    def gather_heads(m):
        total = jnp.where(lane_head == 0, m[:BLOCK], 0.0)
        for h in range(1, GROUP):
            total = jnp.where(lane_head == h, m[h * BLOCK : (h + 1) * BLOCK], total)
        return total

    for b in range(NB):
        keys = pl.ds(b * KEYS, KEYS)
        own = slice(b * BLOCK, (b + 1) * BLOCK)
        kf = k_ref[keys, :].astype(F32)
        norm2 = split_dot(head_pick, kf * kf, NT, 1)
        inv_k = 1.0 / jnp.sqrt(norm2 + head_eps)
        allowed = (seen_ref[b : b + 1, :] > 0.0) | diagonal
        mask = jnp.concatenate([allowed] * GROUP, axis=0)
        for g in range(HEADS // GROUP):
            lanes = slice(g * GL, (g + 1) * GL)
            qm = spread(queries[own, lanes])
            gm = spread(grad_attn[own, lanes])
            k4 = k_ref[keys, lanes]
            v4 = v_ref[keys, lanes]
            qf = qm.astype(F32)
            inv_q = 1.0 / jnp.sqrt(jnp.sum(qf * qf, axis=1, keepdims=True) + head_eps)
            sharp = jnp.concatenate(
                [jnp.full((BLOCK, 1), sharp_ref[g * GROUP + h], F32) for h in range(GROUP)], axis=0
            )
            ik = inv_k[g * GROUP : (g + 1) * GROUP]
            ik_rows = jnp.concatenate(
                [jnp.broadcast_to(ik[h : h + 1], (BLOCK, KEYS)) for h in range(GROUP)], axis=0
            )
            factor = (sharp * inv_q) * ik_rows
            scores = factor * dot(qm, k4, NT)
            expo = jnp.where(mask, jnp.exp(scores), 0.0)
            prob = expo * (1.0 / jnp.sum(expo, axis=1, keepdims=True))
            prob_b = prob.astype(BF16)
            att_ref[own, lanes] = gather_heads(dot(prob_b, v4, NN)).astype(BF16)
            dprob = dot(gm, v4, NT)
            delta = jnp.sum(prob * dprob, axis=1, keepdims=True)
            dscore = prob * (dprob - delta)
            weighted = (factor * dscore).astype(BF16)
            score_grad = scores * dscore
            row_terms = jnp.sum(score_grad, axis=1, keepdims=True)
            gq = dot(weighted, k4, NN) - (inv_q * inv_q * row_terms) * qf
            gq_ref[own, lanes] = gather_heads(gq).astype(BF16)
            col_terms = jnp.concatenate(
                [
                    jnp.sum(score_grad[h * BLOCK : (h + 1) * BLOCK], axis=0, keepdims=True)
                    for h in range(GROUP)
                ],
                axis=0,
            )
            coef = ik * ik * col_terms
            coef = jnp.concatenate([coef] + [jnp.zeros_like(coef)] * 3, axis=0)
            coef = split_dot(coef, group_pick, TN, 0)
            gk = dot(weighted, qm, TN) - coef * k4.astype(F32)
            gkv_ref[keys, g * GL : (g + 1) * GL] = gk.astype(BF16)
            gkv_ref[keys, HDT + g * GL : HDT + (g + 1) * GL] = dot(prob_b, gm, TN).astype(BF16)

    gh_ref[...] = dot(gkv_ref[...], w_ref[:, HDT : 3 * HDT], NT)
    gq_hidden = dot(gq_ref[...], w_ref[:, :HDT], NT)
    for t in range(ITEMS):
        rows = pl.ds(t * BLOCK, BLOCK)
        hidden = gh_ref[rows, :]
        b = t // SLOTS
        if t % SLOTS == 0:
            hidden = hidden + gq_hidden[b * BLOCK : (b + 1) * BLOCK]
        grad = hidden * gain
        normed = normed_ref[rows, :]
        m1 = jnp.mean(grad, axis=1, keepdims=True)
        m2 = jnp.mean(grad * normed, axis=1, keepdims=True)
        grad = rstd_ref[rows, 0:1] * (grad - m1 - normed * m2)
        if t % SLOTS == 0:
            grad = grad + up[b * BLOCK : (b + 1) * BLOCK].astype(F32)
        xn_ref[rows, :] = grad.astype(BF16)
    for q in range(4):
        left, right = quarter(q)
        x = jnp.concatenate(
            [xn_ref[t * BLOCK + q * QB : t * BLOCK + (q + 1) * QB, :] for t in range(ITEMS)], axis=0
        )
        x = dot(back, x, NN).astype(BF16)
        out_ref[left, :] = x[:, :HALF]
        out_ref[right, :] = x[:, HALF:]


def output_kernel(att_ref, own_ref, wo_ref, out_ref):
    out = own_ref[...].astype(F32) + dot(att_ref[...], wo_ref[...], NT)
    out_ref[...] = rolled(out.astype(BF16))


def call(kernel, outs, args, specs, flops, scratch=(), limit=8, out_spec=VM):
    place = pltpu.HBM if out_spec is HB_SPEC else jax.ShapeDtypeStruct
    moved = sum(a.size * a.dtype.itemsize for a in args)
    moved += sum(2 * o[0] * o[1] for o in outs)
    if flops == 0:
        moved = 0
    args = [
        pltpu.with_memory_space_constraint(a, pltpu.HBM) if spec is HB_SPEC else a
        for a, spec in zip(args, specs)
    ]
    return pl.pallas_call(
        kernel,
        out_shape=[place(o[:2], o[2] if len(o) > 2 else BF16) for o in outs],
        in_specs=specs,
        out_specs=[out_spec] * len(outs),
        scratch_shapes=list(scratch),
        compiler_params=pltpu.CompilerParams(vmem_limit_bytes=limit * 2**20),
        cost_estimate=pl.CostEstimate(flops=flops, bytes_accessed=moved, transcendentals=0),
    )(*args)


def main_call(sharpness_coefficient, arrived, weights, upstream_derivative, gain, seen):
    return call(
        main_kernel,
        [(SHARDS * PACK, HALF), (TOK, HDT), (TOK, D), (D, HDT)],
        (
            sharpness_coefficient,
            arrived,
            weights,
            upstream_derivative,
            gain,
            seen,
        ),
        [SM, VM, HB_SPEC, HB_SPEC, VM, VM],
        4 * 10**9,
        scratch=[
            pltpu.VMEM((D, 3 * HDT), BF16),
            pltpu.VMEM((TOK, D), BF16),
            pltpu.SemaphoreType.DMA((3,)),
            pltpu.VMEM((ROWS, D), F32),
            pltpu.VMEM((ROWS, 128), F32),
            pltpu.VMEM((ROWS, D), BF16),
            pltpu.VMEM((ROWS, HDT), BF16),
            pltpu.VMEM((ROWS, HDT), BF16),
            pltpu.VMEM((ROWS, D), BF16),
            pltpu.VMEM((TOK, HDT), BF16),
            pltpu.VMEM((ROWS, D), F32),
        ],
        limit=40,
    )


def body(
    embedded_pieces,
    morton_arrangement,
    unhidden_indicator,
    bordering_tiles,
    bordering_tally,
    standardizer_multiplier,
    sharpness_coefficient,
    probe_projector,
    lookup_projector,
    content_projector,
    result_projector,
    upstream_derivative,
):
    me = lax.axis_index("tok")
    side = (me // (SHARDS // 2)).reshape(1).astype(jnp.int32)
    column = SHARDS // 4
    partner = [(i, (3 - i // column) * column + i % column) for i in range(SHARDS)]

    order = morton_arrangement[0]
    keep, send, share = call(
        arrange_kernel,
        [(TOK, HALF)] * 2 + [(SHARE, 4 * HDT)],
        (
            side,
            order,
            embedded_pieces[0],
            probe_projector,
            lookup_projector,
            content_projector,
            result_projector.T,
        ),
        [SM] + [HB_SPEC] * 6,
        2 * TOK * TOK * D,
        scratch=[
            pltpu.VMEM((1, TOK), jnp.int32),
            pltpu.VMEM((TOK, D), BF16),
            pltpu.SemaphoreType.DMA((6,)),
        ],
    )
    weights = lax.all_gather(share, "fsdp", axis=0, tiled=True)
    recv = lax.ppermute(send, "tok", partner)

    lists = bordering_tiles[0].reshape(SHARDS, NB, KN)
    own_blocks = jnp.arange(SHARDS * NB, dtype=jnp.int32).reshape(SHARDS, NB, 1)
    named = jnp.concatenate([own_blocks, lists], axis=2).reshape(SHARDS, ITEMS)
    target = (named % 2) * TOK + (named // 2) * CHUNK
    target = (target[:, :, None] + jnp.arange(CHUNK, dtype=jnp.int32)).reshape(
        1, SHARDS * PACK
    )
    (packed,) = call(
        pack_kernel,
        [(SHARDS * PACK, HALF)],
        (side, target, keep, recv),
        [SM, VM, VM, VM],
        2 * SHARDS * PACK * 2 * TOK * HALF,
    )
    arrived = lax.all_to_all(
        packed.reshape(SHARDS, PACK, HALF), "tok", split_axis=0, concat_axis=0, tiled=True
    ).reshape(SHARDS * PACK, HALF)

    seen_all = unhidden_indicator[0].reshape(SHARDS, NB, BLOCK).astype(F32)
    seen_all = jnp.stack(
        [
            seen_all[:, 0],
            jnp.concatenate([seen_all[:, 1, HB:], seen_all[:, 1, :HB]], axis=1),
        ],
        axis=1,
    ).reshape(SHARDS * NB, BLOCK)
    used = jnp.arange(SLOTS)[None, :] <= bordering_tally[0][:, None]
    used = used.reshape(SHARDS, ITEMS)
    picks = (
        (named[:, :, None] == jnp.arange(SHARDS * NB)) & used[:, :, None]
    ).astype(F32)
    picks = jnp.sum(picks * (jnp.arange(SHARDS) == me)[:, None, None], axis=0)
    seen = jnp.dot(picks, seen_all).reshape(NB, KEYS)

    leaving, attended, own, out_weight = main_call(
        sharpness_coefficient,
        arrived,
        weights,
        upstream_derivative[0],
        standardizer_multiplier.reshape(1, D),
        seen,
    )
    returned = lax.all_to_all(
        leaving.reshape(SHARDS, PACK, HALF), "tok", split_axis=0, concat_axis=0, tiled=True
    ).reshape(SHARDS * PACK, HALF)
    (layer_out,) = call(
        output_kernel,
        [(TOK, D)],
        (attended, own, out_weight),
        [VM] * 3,
        2 * TOK * HDT * D,
    )
    keep, send = call(
        collect_kernel,
        [(TOK, HALF)] * 2,
        (side, target, returned),
        [SM, VM, VM],
        2 * SHARDS * PACK * 2 * TOK * HALF,
    )
    recv = lax.ppermute(send, "tok", partner)
    (grad_tokens,) = call(
        restore_kernel,
        [(TOK, D)],
        (side, order, keep, recv),
        [SM, VM, VM, VM],
        2 * TOK * TOK * D,
    )
    return (layer_out[None], grad_tokens[None])


def solution(mesh):
    placed = (
        P("fsdp", "tok", None),
        P("fsdp", "tok", None),
        P("fsdp", None),
        P("fsdp", None, None),
        P("fsdp", None),
        P(),
        P(),
        P("fsdp", None),
        P("fsdp", None),
        P("fsdp", None),
        P(None, "fsdp"),
        P("fsdp", "tok", None),
    )
    return jax.shard_map(
        body,
        mesh=mesh,
        in_specs=placed,
        out_specs=(P("fsdp", "tok", None), P("fsdp", "tok", None)),
        check_vma=False,
    )
```

```python
import jax
import jax.numpy as jnp
from jax import lax
from jax.experimental import pallas as pl
from jax.experimental.pallas import tpu as pltpu
from jax.sharding import PartitionSpec as P

HEADS = 8
HEAD_DIM = 64
BLOCK = 64
HB = BLOCK // 2
KN = 4
D = 1024
HDT = 512
SHARDS = 32
TOK = 128
NB = 2
CHUNK = 4
SLOTS = 1 + KN
ITEMS = NB * SLOTS
ROWS = ITEMS * BLOCK
KEYS = SLOTS * BLOCK
HALF = D // 2
QB = BLOCK // 4
QROWS = ROWS // 4
FAR = ROWS + ROWS // 2
PACK = ITEMS * CHUNK
GROUP = 4
GL = GROUP * HEAD_DIM
GR = GROUP * BLOCK

CHIPS = 8
SHARE = 64
CHIP = 2 * SHARE
HOPS = 3

norm_eps = 1e-05
head_eps = 1e-06
F32 = jnp.float32
BF16 = jnp.bfloat16
VM = pl.BlockSpec(memory_space=pltpu.VMEM)
SM = pl.BlockSpec(memory_space=pltpu.SMEM)
ANY = pl.BlockSpec(memory_space=pl.ANY)
HB_SPEC = pl.BlockSpec(memory_space=pltpu.HBM)
NN = (((1,), (0,)), ((), ()))
NT = (((1,), (1,)), ((), ()))
TN = (((0,), (0,)), ((), ()))


def dot(a, b, dims, **kw):
    return lax.dot_general(a, b, dims, preferred_element_type=F32, **kw)


def rolled(m):
    return jnp.concatenate([m[:BLOCK], m[BLOCK + HB :], m[BLOCK : BLOCK + HB]], axis=0)


def split_dot(a, b, dims, which):
    exact = a if which == 0 else b
    high = exact.astype(BF16)
    low = (exact - high.astype(F32)).astype(BF16)
    if which == 0:
        return dot(high, b, dims) + dot(low, b, dims)
    return dot(a, high, dims) + dot(a, low, dims)


def one_hot(row_ref, rows):
    idx = row_ref[...]
    iota = lax.broadcasted_iota(jnp.int32, (rows, idx.shape[1]), 0)
    return jnp.where(iota == idx, 1.0, 0.0).astype(BF16)


def arrange_kernel(
    side_ref,
    order_hbm,
    x_hbm,
    wq_hbm,
    wk_hbm,
    wv_hbm,
    wo_hbm,
    keep_ref,
    send_ref,
    share_ref,
    order_ref,
    x_ref,
    sems,
):
    copies = [
        pltpu.make_async_copy(x_hbm, x_ref, sems.at[0]),
        pltpu.make_async_copy(order_hbm, order_ref, sems.at[1]),
    ]
    for n, part in enumerate((wq_hbm, wk_hbm, wv_hbm, wo_hbm)):
        lanes = pl.ds(n * HDT, HDT)
        copies.append(pltpu.make_async_copy(part, share_ref.at[:, lanes], sems.at[2 + n]))
    for copy in copies:
        copy.start()
    for copy in copies:
        copy.wait()
    a = dot(one_hot(order_ref, TOK), x_ref[...], TN).astype(BF16)
    lower = side_ref[0] == 0
    left, right = a[:, :HALF], a[:, HALF:]
    keep_ref[...] = jnp.where(lower, left, right)
    send_ref[...] = jnp.where(lower, right, left)


def stack_kernel(*refs):
    out_ref, sems = refs[-2:]
    copies, at = [], 0
    for n, ref in enumerate(refs[:-2]):
        rows = ref.shape[0]
        copies.append(pltpu.make_async_copy(ref, out_ref.at[pl.ds(at, rows), :], sems.at[n]))
        at += rows
    for copy in copies:
        copy.start()
    for copy in copies:
        copy.wait()


def pack_kernel(side_ref, target_ref, keep_ref, recv_ref, out_ref):
    lower = side_ref[0] == 0
    keep, recv = keep_ref[...], recv_ref[...]
    table = jnp.concatenate(
        [jnp.where(lower, keep, recv), jnp.where(lower, recv, keep)], axis=0
    )
    out_ref[...] = dot(one_hot(target_ref, 2 * TOK), table, TN).astype(BF16)


def collect_kernel(side_ref, target_ref, in_ref, keep_ref, send_ref):
    total = dot(one_hot(target_ref, 2 * TOK), in_ref[...], NN).astype(BF16)
    lower = side_ref[0] == 0
    even, odd = total[:TOK], total[TOK:]
    keep_ref[...] = jnp.where(lower, even, odd)
    send_ref[...] = jnp.where(lower, odd, even)


def restore_kernel(side_ref, order_ref, keep_ref, recv_ref, out_ref):
    lower = side_ref[0] == 0
    keep, recv = keep_ref[...], recv_ref[...]
    both = jnp.concatenate(
        [jnp.where(lower, keep, recv), jnp.where(lower, recv, keep)], axis=1
    )
    out_ref[...] = dot(one_hot(order_ref, TOK), both, NN).astype(BF16)


def source(dest):
    return (dest % QB // CHUNK) * PACK + (dest // QB) * CHUNK + dest % CHUNK


def quarter(q):
    right = FAR + q * QROWS if q < 2 else ROWS + (q - 2) * QROWS
    return slice(q * QROWS, (q + 1) * QROWS), slice(right, right + QROWS)


def main_kernel(
    sharp_ref,
    place_ref,
    in_ref,
    chip_any,
    mine_any,
    other_any,
    up_hbm,
    gain_ref,
    seen_ref,
    out_ref,
    att_ref,
    own_ref,
    wo_ref,
    w_ref,
    up_ref,
    sems,
    normed_ref,
    rstd_ref,
    xn_ref,
    k_ref,
    v_ref,
    gkv_ref,
    gq_ref,
    gh_ref,
):
    copies = [pltpu.make_async_copy(up_hbm, up_ref, sems.at[0])]

    def bring(part, at, chip, rows, first):
        chip = lax.rem(chip + CHIPS, CHIPS)
        dst = pl.ds(pl.multiple_of(chip * CHIP + first, SHARE), rows)
        src = pl.ds(at, rows)
        for lanes, ref in ((pl.ds(0, 3 * HDT), w_ref), (pl.ds(3 * HDT, HDT), wo_ref)):
            copies.append(
                pltpu.make_async_copy(part.at[src, lanes], ref.at[dst, :], sems.at[len(copies)])
            )

    y, core = place_ref[0], place_ref[1]
    bring(chip_any, 0, y, CHIP, 0)
    for part, side in ((mine_any, core), (other_any, 1 - core)):
        for hop in range(HOPS):
            bring(part, hop * CHIP, y + (2 * side - 1) * (hop + 1), CHIP, 0)
        bring(part, HOPS * CHIP, y + CHIPS // 2, SHARE, side * SHARE)
    for copy in copies:
        copy.start()
    shape = (QROWS, QROWS)
    row = source(lax.broadcasted_iota(jnp.int32, (QROWS, 1), 0))
    perm = jnp.where(row == lax.broadcasted_iota(jnp.int32, shape, 1), 1.0, 0.0).astype(BF16)
    column = source(lax.broadcasted_iota(jnp.int32, (1, QROWS), 1))
    back = jnp.where(column == lax.broadcasted_iota(jnp.int32, shape, 0), 1.0, 0.0).astype(BF16)
    for q in range(4):
        left, right = quarter(q)
        x_in = jnp.concatenate([in_ref[left, :], in_ref[right, :]], axis=1)
        x = dot(perm, x_in, NN)
        for t in range(ITEMS):
            at = t * BLOCK + q * QB
            normed_ref[at : at + QB, :] = x[t * QB : (t + 1) * QB]
    gain = gain_ref[...].astype(F32)
    for t in range(ITEMS):
        rows = pl.ds(t * BLOCK, BLOCK)
        x = normed_ref[rows, :]
        if t % SLOTS == 0:
            own_ref[pl.ds(t // SLOTS * BLOCK, BLOCK), :] = x.astype(BF16)
        centered = x - jnp.mean(x, axis=1, keepdims=True)
        rstd = 1.0 / jnp.sqrt(jnp.mean(centered * centered, axis=1, keepdims=True) + norm_eps)
        normed = centered * rstd
        normed_ref[rows, :] = normed
        rstd_ref[rows, :] = jnp.broadcast_to(rstd, (BLOCK, 128))
        xn_ref[rows, :] = (normed * gain).astype(BF16)
    for copy in copies:
        copy.wait()
    xn = xn_ref[...]
    k_ref[...] = dot(xn, w_ref[:, HDT : 2 * HDT], NN).astype(BF16)
    v_ref[...] = dot(xn, w_ref[:, 2 * HDT : 3 * HDT], NN).astype(BF16)
    xn_own = jnp.concatenate([xn_ref[pl.ds(b * KEYS, BLOCK), :] for b in range(NB)], axis=0)
    queries = dot(xn_own, w_ref[:, :HDT], NN).astype(BF16)
    up = rolled(up_ref[...])
    grad_attn = dot(up, wo_ref[...], NN).astype(BF16)

    lane_head = lax.broadcasted_iota(jnp.int32, (BLOCK, GL), 1) // HEAD_DIM
    def picks(shape):
        hit = lax.broadcasted_iota(jnp.int32, shape, 1) // HEAD_DIM == lax.broadcasted_iota(
            jnp.int32, shape, 0
        )
        return jnp.where(hit, 1.0, 0.0).astype(BF16)

    head_pick = picks((16, HDT))
    group_pick = picks((16, GL))
    diagonal = lax.broadcasted_iota(jnp.int32, (BLOCK, KEYS), 0) == lax.broadcasted_iota(
        jnp.int32, (BLOCK, KEYS), 1
    )

    def spread(m):
        return jnp.concatenate(
            [jnp.where(lane_head == h, m, jnp.zeros_like(m)) for h in range(GROUP)], axis=0
        )

    def gather_heads(m):
        total = jnp.where(lane_head == 0, m[:BLOCK], 0.0)
        for h in range(1, GROUP):
            total = jnp.where(lane_head == h, m[h * BLOCK : (h + 1) * BLOCK], total)
        return total

    for b in range(NB):
        keys = pl.ds(b * KEYS, KEYS)
        own = slice(b * BLOCK, (b + 1) * BLOCK)
        kf = k_ref[keys, :].astype(F32)
        norm2 = split_dot(head_pick, kf * kf, NT, 1)
        inv_k = 1.0 / jnp.sqrt(norm2 + head_eps)
        allowed = (seen_ref[b : b + 1, :] > 0.0) | diagonal
        mask = jnp.concatenate([allowed] * GROUP, axis=0)
        for g in range(HEADS // GROUP):
            lanes = slice(g * GL, (g + 1) * GL)
            qm = spread(queries[own, lanes])
            gm = spread(grad_attn[own, lanes])
            k4 = k_ref[keys, lanes]
            v4 = v_ref[keys, lanes]
            qf = qm.astype(F32)
            inv_q = 1.0 / jnp.sqrt(jnp.sum(qf * qf, axis=1, keepdims=True) + head_eps)
            sharp = jnp.concatenate(
                [jnp.full((BLOCK, 1), sharp_ref[g * GROUP + h], F32) for h in range(GROUP)], axis=0
            )
            ik = inv_k[g * GROUP : (g + 1) * GROUP]
            ik_rows = jnp.concatenate(
                [jnp.broadcast_to(ik[h : h + 1], (BLOCK, KEYS)) for h in range(GROUP)], axis=0
            )
            factor = (sharp * inv_q) * ik_rows
            scores = factor * dot(qm, k4, NT)
            expo = jnp.where(mask, jnp.exp(scores), 0.0)
            prob = expo * (1.0 / jnp.sum(expo, axis=1, keepdims=True))
            prob_b = prob.astype(BF16)
            att_ref[own, lanes] = gather_heads(dot(prob_b, v4, NN)).astype(BF16)
            dprob = dot(gm, v4, NT)
            delta = jnp.sum(prob * dprob, axis=1, keepdims=True)
            dscore = prob * (dprob - delta)
            weighted = (factor * dscore).astype(BF16)
            score_grad = scores * dscore
            row_terms = jnp.sum(score_grad, axis=1, keepdims=True)
            gq = dot(weighted, k4, NN) - (inv_q * inv_q * row_terms) * qf
            gq_ref[own, lanes] = gather_heads(gq).astype(BF16)
            col_terms = jnp.concatenate(
                [
                    jnp.sum(score_grad[h * BLOCK : (h + 1) * BLOCK], axis=0, keepdims=True)
                    for h in range(GROUP)
                ],
                axis=0,
            )
            coef = ik * ik * col_terms
            coef = jnp.concatenate([coef] + [jnp.zeros_like(coef)] * 3, axis=0)
            coef = split_dot(coef, group_pick, TN, 0)
            gk = dot(weighted, qm, TN) - coef * k4.astype(F32)
            gkv_ref[keys, g * GL : (g + 1) * GL] = gk.astype(BF16)
            gkv_ref[keys, HDT + g * GL : HDT + (g + 1) * GL] = dot(prob_b, gm, TN).astype(BF16)

    gh_ref[...] = dot(gkv_ref[...], w_ref[:, HDT : 3 * HDT], NT)
    gq_hidden = dot(gq_ref[...], w_ref[:, :HDT], NT)
    for t in range(ITEMS):
        rows = pl.ds(t * BLOCK, BLOCK)
        hidden = gh_ref[rows, :]
        b = t // SLOTS
        if t % SLOTS == 0:
            hidden = hidden + gq_hidden[b * BLOCK : (b + 1) * BLOCK]
        grad = hidden * gain
        normed = normed_ref[rows, :]
        m1 = jnp.mean(grad, axis=1, keepdims=True)
        m2 = jnp.mean(grad * normed, axis=1, keepdims=True)
        grad = rstd_ref[rows, 0:1] * (grad - m1 - normed * m2)
        if t % SLOTS == 0:
            grad = grad + up[b * BLOCK : (b + 1) * BLOCK].astype(F32)
        xn_ref[rows, :] = grad.astype(BF16)
    for q in range(4):
        left, right = quarter(q)
        x = jnp.concatenate(
            [xn_ref[t * BLOCK + q * QB : t * BLOCK + (q + 1) * QB, :] for t in range(ITEMS)], axis=0
        )
        x = dot(back, x, NN).astype(BF16)
        out_ref[left, :] = x[:, :HALF]
        out_ref[right, :] = x[:, HALF:]


def output_kernel(att_ref, own_ref, wo_ref, out_ref):
    out = own_ref[...].astype(F32) + dot(att_ref[...], wo_ref[...], NT)
    out_ref[...] = rolled(out.astype(BF16))


def call(kernel, outs, args, specs, flops, scratch=(), limit=8, out_spec=VM):
    place = pltpu.HBM if out_spec is HB_SPEC else jax.ShapeDtypeStruct
    moved = sum(a.size * a.dtype.itemsize for a in args)
    moved += sum(2 * o[0] * o[1] for o in outs)
    if flops == 0:
        moved = 0
    args = [
        pltpu.with_memory_space_constraint(a, pltpu.HBM) if spec is HB_SPEC else a
        for a, spec in zip(args, specs)
    ]
    return pl.pallas_call(
        kernel,
        out_shape=[place(o[:2], o[2] if len(o) > 2 else BF16) for o in outs],
        in_specs=specs,
        out_specs=[out_spec] * len(outs),
        scratch_shapes=list(scratch),
        compiler_params=pltpu.CompilerParams(vmem_limit_bytes=limit * 2**20),
        cost_estimate=pl.CostEstimate(flops=flops, bytes_accessed=moved, transcendentals=0),
    )(*args)


def gather_weights(share, place):
    members = 2 * CHIPS
    sibling = [(i, i ^ 1) for i in range(members)]

    def onward(part, hops):
        pairs = [(i, (i + hops * (2 - 4 * (i % 2))) % members) for i in range(members)]
        return lax.ppermute(part, "fsdp", pairs)

    first = place[1] == 0
    beside = lax.ppermute(share, "fsdp", sibling)
    chip = jnp.concatenate(
        [jnp.where(first, share, beside), jnp.where(first, beside, share)], axis=0
    )
    near, far = onward(chip, 1), onward(chip, 2)
    half = jnp.where(first, far[:SHARE], far[SHARE:])
    pieces = [near, far, onward(far, 1), onward(half, 2)]
    (mine,) = call(
        stack_kernel,
        [(HOPS * CHIP + SHARE, 4 * HDT)],
        pieces,
        [HB_SPEC] * (HOPS + 1),
        0,
        scratch=[pltpu.SemaphoreType.DMA((HOPS + 1,))],
    )
    return chip, mine, lax.ppermute(mine, "fsdp", sibling)


def main_call(sharpness_coefficient, place, arrived, chip, mine, other, upstream_derivative, gain, seen):
    return call(
        main_kernel,
        [(SHARDS * PACK, HALF), (TOK, HDT), (TOK, D), (D, HDT)],
        (
            sharpness_coefficient,
            place,
            arrived,
            chip,
            mine,
            other,
            upstream_derivative,
            gain,
            seen,
        ),
        [SM, SM, VM, HB_SPEC, ANY, ANY, HB_SPEC, VM, VM],
        4 * 10**9,
        scratch=[
            pltpu.VMEM((D, 3 * HDT), BF16),
            pltpu.VMEM((TOK, D), BF16),
            pltpu.SemaphoreType.DMA((7 + 4 * (HOPS + 1),)),
            pltpu.VMEM((ROWS, D), F32),
            pltpu.VMEM((ROWS, 128), F32),
            pltpu.VMEM((ROWS, D), BF16),
            pltpu.VMEM((ROWS, HDT), BF16),
            pltpu.VMEM((ROWS, HDT), BF16),
            pltpu.VMEM((ROWS, D), BF16),
            pltpu.VMEM((TOK, HDT), BF16),
            pltpu.VMEM((ROWS, D), F32),
        ],
        limit=40,
    )


def body(
    embedded_pieces,
    morton_arrangement,
    unhidden_indicator,
    bordering_tiles,
    bordering_tally,
    standardizer_multiplier,
    sharpness_coefficient,
    probe_projector,
    lookup_projector,
    content_projector,
    result_projector,
    upstream_derivative,
):
    me = lax.axis_index("tok")
    side = (me // (SHARDS // 2)).reshape(1).astype(jnp.int32)
    column = SHARDS // 4
    partner = [(i, (3 - i // column) * column + i % column) for i in range(SHARDS)]

    order = morton_arrangement[0]
    keep, send, share = call(
        arrange_kernel,
        [(TOK, HALF)] * 2 + [(SHARE, 4 * HDT)],
        (
            side,
            order,
            embedded_pieces[0],
            probe_projector,
            lookup_projector,
            content_projector,
            result_projector.T,
        ),
        [SM] + [HB_SPEC] * 6,
        2 * TOK * TOK * D,
        scratch=[
            pltpu.VMEM((1, TOK), jnp.int32),
            pltpu.VMEM((TOK, D), BF16),
            pltpu.SemaphoreType.DMA((6,)),
        ],
    )
    member = lax.axis_index("fsdp").astype(jnp.int32)
    place = jnp.stack([member // 2, member % 2])
    chip, mine, other = gather_weights(share, place)
    recv = lax.ppermute(send, "tok", partner)

    lists = bordering_tiles[0].reshape(SHARDS, NB, KN)
    own_blocks = jnp.arange(SHARDS * NB, dtype=jnp.int32).reshape(SHARDS, NB, 1)
    named = jnp.concatenate([own_blocks, lists], axis=2).reshape(SHARDS, ITEMS)
    target = (named % 2) * TOK + (named // 2) * CHUNK
    target = (target[:, :, None] + jnp.arange(CHUNK, dtype=jnp.int32)).reshape(
        1, SHARDS * PACK
    )
    (packed,) = call(
        pack_kernel,
        [(SHARDS * PACK, HALF)],
        (side, target, keep, recv),
        [SM, VM, VM, VM],
        2 * SHARDS * PACK * 2 * TOK * HALF,
    )
    arrived = lax.all_to_all(
        packed.reshape(SHARDS, PACK, HALF), "tok", split_axis=0, concat_axis=0, tiled=True
    ).reshape(SHARDS * PACK, HALF)

    seen_all = unhidden_indicator[0].reshape(SHARDS, NB, BLOCK).astype(F32)
    seen_all = jnp.stack(
        [
            seen_all[:, 0],
            jnp.concatenate([seen_all[:, 1, HB:], seen_all[:, 1, :HB]], axis=1),
        ],
        axis=1,
    ).reshape(SHARDS * NB, BLOCK)
    used = jnp.arange(SLOTS)[None, :] <= bordering_tally[0][:, None]
    used = used.reshape(SHARDS, ITEMS)
    picks = (
        (named[:, :, None] == jnp.arange(SHARDS * NB)) & used[:, :, None]
    ).astype(F32)
    picks = jnp.sum(picks * (jnp.arange(SHARDS) == me)[:, None, None], axis=0)
    seen = jnp.dot(picks, seen_all).reshape(NB, KEYS)

    leaving, attended, own, out_weight = main_call(
        sharpness_coefficient,
        place,
        arrived,
        chip,
        mine,
        other,
        upstream_derivative[0],
        standardizer_multiplier.reshape(1, D),
        seen,
    )
    returned = lax.all_to_all(
        leaving.reshape(SHARDS, PACK, HALF), "tok", split_axis=0, concat_axis=0, tiled=True
    ).reshape(SHARDS * PACK, HALF)
    (layer_out,) = call(
        output_kernel,
        [(TOK, D)],
        (attended, own, out_weight),
        [VM] * 3,
        2 * TOK * HDT * D,
    )
    keep, send = call(
        collect_kernel,
        [(TOK, HALF)] * 2,
        (side, target, returned),
        [SM, VM, VM],
        2 * SHARDS * PACK * 2 * TOK * HALF,
    )
    recv = lax.ppermute(send, "tok", partner)
    (grad_tokens,) = call(
        restore_kernel,
        [(TOK, D)],
        (side, order, keep, recv),
        [SM, VM, VM, VM],
        2 * TOK * TOK * D,
    )
    return (layer_out[None], grad_tokens[None])


def solution(mesh):
    placed = (
        P("fsdp", "tok", None),
        P("fsdp", "tok", None),
        P("fsdp", None),
        P("fsdp", None, None),
        P("fsdp", None),
        P(),
        P(),
        P("fsdp", None),
        P("fsdp", None),
        P("fsdp", None),
        P(None, "fsdp"),
        P("fsdp", "tok", None),
    )
    return jax.shard_map(
        body,
        mesh=mesh,
        in_specs=placed,
        out_specs=(P("fsdp", "tok", None), P("fsdp", "tok", None)),
        check_vma=False,
    )
```

```python
import jax
import jax.numpy as jnp
from jax import lax
from jax.experimental import pallas as pl
from jax.experimental.pallas import tpu as pltpu
from jax.sharding import PartitionSpec as P

HEADS = 8
HEAD_DIM = 64
BLOCK = 64
HB = BLOCK // 2
KN = 4
D = 1024
HDT = 512
SHARDS = 32
TOK = 128
NB = 2
CHUNK = 4
SLOTS = 1 + KN
ITEMS = NB * SLOTS
ROWS = ITEMS * BLOCK
KEYS = SLOTS * BLOCK
HALF = D // 2
QB = BLOCK // 4
QROWS = ROWS // 4
FAR = ROWS + ROWS // 2
PACK = ITEMS * CHUNK
GROUP = 4
GL = GROUP * HEAD_DIM
GR = GROUP * BLOCK

CHIPS = 8
SHARE = 64
CHIP = 2 * SHARE
HOPS = 3

norm_eps = 1e-05
head_eps = 1e-06
F32 = jnp.float32
BF16 = jnp.bfloat16
VM = pl.BlockSpec(memory_space=pltpu.VMEM)
SM = pl.BlockSpec(memory_space=pltpu.SMEM)
ANY = pl.BlockSpec(memory_space=pl.ANY)
HB_SPEC = pl.BlockSpec(memory_space=pltpu.HBM)
NN = (((1,), (0,)), ((), ()))
NT = (((1,), (1,)), ((), ()))
TN = (((0,), (0,)), ((), ()))


def dot(a, b, dims, **kw):
    return lax.dot_general(a, b, dims, preferred_element_type=F32, **kw)


def rolled(m):
    return jnp.concatenate([m[:BLOCK], m[BLOCK + HB :], m[BLOCK : BLOCK + HB]], axis=0)


def split_dot(a, b, dims, which):
    exact = a if which == 0 else b
    high = exact.astype(BF16)
    low = (exact - high.astype(F32)).astype(BF16)
    if which == 0:
        return dot(high, b, dims) + dot(low, b, dims)
    return dot(a, high, dims) + dot(a, low, dims)


def one_hot(idx, rows):
    iota = lax.broadcasted_iota(jnp.int32, (rows, idx.shape[1]), 0)
    return jnp.where(iota == idx, 1.0, 0.0).astype(BF16)


def arrange_kernel(
    side_ref,
    order_hbm,
    x_hbm,
    wq_hbm,
    wk_hbm,
    wv_hbm,
    wo_hbm,
    keep_ref,
    send_ref,
    share_ref,
    order_ref,
    x_ref,
    sems,
):
    copies = [
        pltpu.make_async_copy(x_hbm, x_ref, sems.at[0]),
        pltpu.make_async_copy(order_hbm, order_ref, sems.at[1]),
    ]
    for n, part in enumerate((wq_hbm, wk_hbm, wv_hbm, wo_hbm)):
        lanes = pl.ds(n * HDT, HDT)
        copies.append(pltpu.make_async_copy(part, share_ref.at[:, lanes], sems.at[2 + n]))
    for copy in copies:
        copy.start()
    for copy in copies:
        copy.wait()
    a = dot(one_hot(order_ref[...], TOK), x_ref[...], TN).astype(BF16)
    lower = side_ref[0] == 0
    left, right = a[:, :HALF], a[:, HALF:]
    keep_ref[...] = jnp.where(lower, left, right)
    send_ref[...] = jnp.where(lower, right, left)


def stack_kernel(*refs):
    out_ref, sems = refs[-2:]
    copies, at = [], 0
    for n, ref in enumerate(refs[:-2]):
        rows = ref.shape[0]
        copies.append(pltpu.make_async_copy(ref, out_ref.at[pl.ds(at, rows), :], sems.at[n]))
        at += rows
    for copy in copies:
        copy.start()
    for copy in copies:
        copy.wait()


def targets(lists):
    blocks = SHARDS * NB
    row = lax.broadcasted_iota(jnp.int32, (16, blocks), 0)
    named = lax.broadcasted_iota(jnp.int32, (16, blocks), 1)
    for m in range(KN):
        named = jnp.where(row == m + 1, lists[m : m + 1, :], named)
    first = ((named & 1) * TOK + (named >> 1) * CHUNK).astype(F32).astype(BF16)
    column = lax.broadcasted_iota(jnp.int32, (1, SHARDS * PACK), 1)
    item = column % PACK // CHUNK
    block = column // PACK * NB + item // SLOTS
    mine = lax.broadcasted_iota(jnp.int32, (blocks, SHARDS * PACK), 0) == block
    spread = dot(first, jnp.where(mine, 1.0, 0.0).astype(BF16), NN)
    total = (column % CHUNK).astype(F32)
    for m in range(SLOTS):
        total = total + jnp.where(item % SLOTS == m, spread[m : m + 1, :], 0.0)
    return total.astype(jnp.int32)


def target_kernel(lists_ref, target_ref):
    target_ref[...] = targets(lists_ref[...])


def pack_kernel(side_ref, target_ref, keep_ref, recv_ref, out_ref):
    lower = side_ref[0] == 0
    keep, recv = keep_ref[...], recv_ref[...]
    table = jnp.concatenate(
        [jnp.where(lower, keep, recv), jnp.where(lower, recv, keep)], axis=0
    )
    out_ref[...] = dot(one_hot(target_ref[...], 2 * TOK), table, TN).astype(BF16)


def collect_kernel(side_ref, target_ref, in_ref, keep_ref, send_ref):
    total = dot(one_hot(target_ref[...], 2 * TOK), in_ref[...], NN).astype(BF16)
    lower = side_ref[0] == 0
    even, odd = total[:TOK], total[TOK:]
    keep_ref[...] = jnp.where(lower, even, odd)
    send_ref[...] = jnp.where(lower, odd, even)


def restore_kernel(side_ref, order_ref, keep_ref, recv_ref, out_ref):
    lower = side_ref[0] == 0
    keep, recv = keep_ref[...], recv_ref[...]
    both = jnp.concatenate(
        [jnp.where(lower, keep, recv), jnp.where(lower, recv, keep)], axis=1
    )
    out_ref[...] = dot(one_hot(order_ref[...], TOK), both, NN).astype(BF16)


def source(dest):
    return (dest % QB // CHUNK) * PACK + (dest // QB) * CHUNK + dest % CHUNK


def quarter(q):
    right = FAR + q * QROWS if q < 2 else ROWS + (q - 2) * QROWS
    return slice(q * QROWS, (q + 1) * QROWS), slice(right, right + QROWS)


def main_kernel(
    sharp_ref,
    place_ref,
    in_ref,
    chip_any,
    mine_any,
    other_any,
    up_hbm,
    gain_ref,
    seen_ref,
    out_ref,
    att_ref,
    own_ref,
    wo_ref,
    w_ref,
    up_ref,
    sems,
    normed_ref,
    rstd_ref,
    xn_ref,
    k_ref,
    v_ref,
    gkv_ref,
    gq_ref,
    gh_ref,
):
    copies = [pltpu.make_async_copy(up_hbm, up_ref, sems.at[0])]

    def bring(part, at, chip, rows, first):
        chip = lax.rem(chip + CHIPS, CHIPS)
        dst = pl.ds(pl.multiple_of(chip * CHIP + first, SHARE), rows)
        src = pl.ds(at, rows)
        for lanes, ref in ((pl.ds(0, 3 * HDT), w_ref), (pl.ds(3 * HDT, HDT), wo_ref)):
            copies.append(
                pltpu.make_async_copy(part.at[src, lanes], ref.at[dst, :], sems.at[len(copies)])
            )

    y, core = place_ref[0], place_ref[1]
    bring(chip_any, 0, y, CHIP, 0)
    for part, side in ((mine_any, core), (other_any, 1 - core)):
        for hop in range(HOPS):
            bring(part, hop * CHIP, y + (2 * side - 1) * (hop + 1), CHIP, 0)
        bring(part, HOPS * CHIP, y + CHIPS // 2, SHARE, side * SHARE)
    for copy in copies:
        copy.start()
    shape = (QROWS, QROWS)
    row = source(lax.broadcasted_iota(jnp.int32, (QROWS, 1), 0))
    perm = jnp.where(row == lax.broadcasted_iota(jnp.int32, shape, 1), 1.0, 0.0).astype(BF16)
    column = source(lax.broadcasted_iota(jnp.int32, (1, QROWS), 1))
    back = jnp.where(column == lax.broadcasted_iota(jnp.int32, shape, 0), 1.0, 0.0).astype(BF16)
    for q in range(4):
        left, right = quarter(q)
        x_in = jnp.concatenate([in_ref[left, :], in_ref[right, :]], axis=1)
        x = dot(perm, x_in, NN)
        for t in range(ITEMS):
            at = t * BLOCK + q * QB
            normed_ref[at : at + QB, :] = x[t * QB : (t + 1) * QB]
    gain = gain_ref[...].astype(F32)
    for t in range(ITEMS):
        rows = pl.ds(t * BLOCK, BLOCK)
        x = normed_ref[rows, :]
        if t % SLOTS == 0:
            own_ref[pl.ds(t // SLOTS * BLOCK, BLOCK), :] = x.astype(BF16)
        centered = x - jnp.mean(x, axis=1, keepdims=True)
        rstd = 1.0 / jnp.sqrt(jnp.mean(centered * centered, axis=1, keepdims=True) + norm_eps)
        normed = centered * rstd
        normed_ref[rows, :] = normed
        rstd_ref[rows, :] = jnp.broadcast_to(rstd, (BLOCK, 128))
        xn_ref[rows, :] = (normed * gain).astype(BF16)
    for copy in copies:
        copy.wait()
    xn = xn_ref[...]
    k_ref[...] = dot(xn, w_ref[:, HDT : 2 * HDT], NN).astype(BF16)
    v_ref[...] = dot(xn, w_ref[:, 2 * HDT : 3 * HDT], NN).astype(BF16)
    xn_own = jnp.concatenate([xn_ref[pl.ds(b * KEYS, BLOCK), :] for b in range(NB)], axis=0)
    queries = dot(xn_own, w_ref[:, :HDT], NN).astype(BF16)
    up = rolled(up_ref[...])
    grad_attn = dot(up, wo_ref[...], NN).astype(BF16)

    lane_head = lax.broadcasted_iota(jnp.int32, (BLOCK, GL), 1) // HEAD_DIM
    def picks(shape):
        hit = lax.broadcasted_iota(jnp.int32, shape, 1) // HEAD_DIM == lax.broadcasted_iota(
            jnp.int32, shape, 0
        )
        return jnp.where(hit, 1.0, 0.0).astype(BF16)

    head_pick = picks((16, HDT))
    group_pick = picks((16, GL))
    diagonal = lax.broadcasted_iota(jnp.int32, (BLOCK, KEYS), 0) == lax.broadcasted_iota(
        jnp.int32, (BLOCK, KEYS), 1
    )

    def spread(m):
        return jnp.concatenate(
            [jnp.where(lane_head == h, m, jnp.zeros_like(m)) for h in range(GROUP)], axis=0
        )

    def gather_heads(m):
        total = jnp.where(lane_head == 0, m[:BLOCK], 0.0)
        for h in range(1, GROUP):
            total = jnp.where(lane_head == h, m[h * BLOCK : (h + 1) * BLOCK], total)
        return total

    for b in range(NB):
        keys = pl.ds(b * KEYS, KEYS)
        own = slice(b * BLOCK, (b + 1) * BLOCK)
        kf = k_ref[keys, :].astype(F32)
        norm2 = split_dot(head_pick, kf * kf, NT, 1)
        inv_k = 1.0 / jnp.sqrt(norm2 + head_eps)
        allowed = (seen_ref[b : b + 1, :] > 0.0) | diagonal
        mask = jnp.concatenate([allowed] * GROUP, axis=0)
        for g in range(HEADS // GROUP):
            lanes = slice(g * GL, (g + 1) * GL)
            qm = spread(queries[own, lanes])
            gm = spread(grad_attn[own, lanes])
            k4 = k_ref[keys, lanes]
            v4 = v_ref[keys, lanes]
            qf = qm.astype(F32)
            inv_q = 1.0 / jnp.sqrt(jnp.sum(qf * qf, axis=1, keepdims=True) + head_eps)
            sharp = jnp.concatenate(
                [jnp.full((BLOCK, 1), sharp_ref[g * GROUP + h], F32) for h in range(GROUP)], axis=0
            )
            ik = inv_k[g * GROUP : (g + 1) * GROUP]
            ik_rows = jnp.concatenate(
                [jnp.broadcast_to(ik[h : h + 1], (BLOCK, KEYS)) for h in range(GROUP)], axis=0
            )
            factor = (sharp * inv_q) * ik_rows
            scores = factor * dot(qm, k4, NT)
            expo = jnp.where(mask, jnp.exp(scores), 0.0)
            prob = expo * (1.0 / jnp.sum(expo, axis=1, keepdims=True))
            prob_b = prob.astype(BF16)
            att_ref[own, lanes] = gather_heads(dot(prob_b, v4, NN)).astype(BF16)
            dprob = dot(gm, v4, NT)
            delta = jnp.sum(prob * dprob, axis=1, keepdims=True)
            dscore = prob * (dprob - delta)
            weighted = (factor * dscore).astype(BF16)
            score_grad = scores * dscore
            row_terms = jnp.sum(score_grad, axis=1, keepdims=True)
            gq = dot(weighted, k4, NN) - (inv_q * inv_q * row_terms) * qf
            gq_ref[own, lanes] = gather_heads(gq).astype(BF16)
            col_terms = jnp.concatenate(
                [
                    jnp.sum(score_grad[h * BLOCK : (h + 1) * BLOCK], axis=0, keepdims=True)
                    for h in range(GROUP)
                ],
                axis=0,
            )
            coef = ik * ik * col_terms
            coef = jnp.concatenate([coef] + [jnp.zeros_like(coef)] * 3, axis=0)
            coef = split_dot(coef, group_pick, TN, 0)
            gk = dot(weighted, qm, TN) - coef * k4.astype(F32)
            gkv_ref[keys, g * GL : (g + 1) * GL] = gk.astype(BF16)
            gkv_ref[keys, HDT + g * GL : HDT + (g + 1) * GL] = dot(prob_b, gm, TN).astype(BF16)

    gh_ref[...] = dot(gkv_ref[...], w_ref[:, HDT : 3 * HDT], NT)
    gq_hidden = dot(gq_ref[...], w_ref[:, :HDT], NT)
    for t in range(ITEMS):
        rows = pl.ds(t * BLOCK, BLOCK)
        hidden = gh_ref[rows, :]
        b = t // SLOTS
        if t % SLOTS == 0:
            hidden = hidden + gq_hidden[b * BLOCK : (b + 1) * BLOCK]
        grad = hidden * gain
        normed = normed_ref[rows, :]
        m1 = jnp.mean(grad, axis=1, keepdims=True)
        m2 = jnp.mean(grad * normed, axis=1, keepdims=True)
        grad = rstd_ref[rows, 0:1] * (grad - m1 - normed * m2)
        if t % SLOTS == 0:
            grad = grad + up[b * BLOCK : (b + 1) * BLOCK].astype(F32)
        xn_ref[rows, :] = grad.astype(BF16)
    for q in range(4):
        left, right = quarter(q)
        x = jnp.concatenate(
            [xn_ref[t * BLOCK + q * QB : t * BLOCK + (q + 1) * QB, :] for t in range(ITEMS)], axis=0
        )
        x = dot(back, x, NN).astype(BF16)
        out_ref[left, :] = x[:, :HALF]
        out_ref[right, :] = x[:, HALF:]


def output_kernel(att_ref, own_ref, wo_ref, out_ref):
    out = own_ref[...].astype(F32) + dot(att_ref[...], wo_ref[...], NT)
    out_ref[...] = rolled(out.astype(BF16))


def call(kernel, outs, args, specs, flops, scratch=(), limit=8, out_spec=VM):
    place = pltpu.HBM if out_spec is HB_SPEC else jax.ShapeDtypeStruct
    moved = sum(a.size * a.dtype.itemsize for a in args)
    moved += sum(2 * o[0] * o[1] for o in outs)
    if flops == 0:
        moved = 0
    args = [
        pltpu.with_memory_space_constraint(a, pltpu.HBM) if spec is HB_SPEC else a
        for a, spec in zip(args, specs)
    ]
    return pl.pallas_call(
        kernel,
        out_shape=[place(o[:2], o[2] if len(o) > 2 else BF16) for o in outs],
        in_specs=specs,
        out_specs=[out_spec] * len(outs),
        scratch_shapes=list(scratch),
        compiler_params=pltpu.CompilerParams(vmem_limit_bytes=limit * 2**20),
        cost_estimate=pl.CostEstimate(flops=flops, bytes_accessed=moved, transcendentals=0),
    )(*args)


def gather_weights(share, place):
    members = 2 * CHIPS
    sibling = [(i, i ^ 1) for i in range(members)]

    def onward(part, hops):
        pairs = [(i, (i + hops * (2 - 4 * (i % 2))) % members) for i in range(members)]
        return lax.ppermute(part, "fsdp", pairs)

    first = place[1] == 0
    beside = lax.ppermute(share, "fsdp", sibling)
    chip = jnp.concatenate(
        [jnp.where(first, share, beside), jnp.where(first, beside, share)], axis=0
    )
    near, far = onward(chip, 1), onward(chip, 2)
    half = jnp.where(first, far[:SHARE], far[SHARE:])
    pieces = [near, far, onward(far, 1), onward(half, 2)]
    (mine,) = call(
        stack_kernel,
        [(HOPS * CHIP + SHARE, 4 * HDT)],
        pieces,
        [HB_SPEC] * (HOPS + 1),
        0,
        scratch=[pltpu.SemaphoreType.DMA((HOPS + 1,))],
    )
    return chip, mine, lax.ppermute(mine, "fsdp", sibling)


def main_call(sharpness_coefficient, place, arrived, chip, mine, other, upstream_derivative, gain, seen):
    return call(
        main_kernel,
        [(SHARDS * PACK, HALF), (TOK, HDT), (TOK, D), (D, HDT)],
        (
            sharpness_coefficient,
            place,
            arrived,
            chip,
            mine,
            other,
            upstream_derivative,
            gain,
            seen,
        ),
        [SM, SM, VM, HB_SPEC, ANY, ANY, HB_SPEC, VM, VM],
        4 * 10**9,
        scratch=[
            pltpu.VMEM((D, 3 * HDT), BF16),
            pltpu.VMEM((TOK, D), BF16),
            pltpu.SemaphoreType.DMA((7 + 4 * (HOPS + 1),)),
            pltpu.VMEM((ROWS, D), F32),
            pltpu.VMEM((ROWS, 128), F32),
            pltpu.VMEM((ROWS, D), BF16),
            pltpu.VMEM((ROWS, HDT), BF16),
            pltpu.VMEM((ROWS, HDT), BF16),
            pltpu.VMEM((ROWS, D), BF16),
            pltpu.VMEM((TOK, HDT), BF16),
            pltpu.VMEM((ROWS, D), F32),
        ],
        limit=40,
    )


def body(
    embedded_pieces,
    morton_arrangement,
    unhidden_indicator,
    bordering_tiles,
    bordering_tally,
    standardizer_multiplier,
    sharpness_coefficient,
    probe_projector,
    lookup_projector,
    content_projector,
    result_projector,
    upstream_derivative,
):
    me = lax.axis_index("tok")
    side = (me // (SHARDS // 2)).reshape(1).astype(jnp.int32)
    column = SHARDS // 4
    partner = [(i, (3 - i // column) * column + i % column) for i in range(SHARDS)]

    order = morton_arrangement[0]
    keep, send, share = call(
        arrange_kernel,
        [(TOK, HALF)] * 2 + [(SHARE, 4 * HDT)],
        (
            side,
            order,
            embedded_pieces[0],
            probe_projector,
            lookup_projector,
            content_projector,
            result_projector.T,
        ),
        [SM] + [HB_SPEC] * 6,
        2 * TOK * TOK * D,
        scratch=[
            pltpu.VMEM((1, TOK), jnp.int32),
            pltpu.VMEM((TOK, D), BF16),
            pltpu.SemaphoreType.DMA((6,)),
        ],
    )
    member = lax.axis_index("fsdp").astype(jnp.int32)
    place = jnp.stack([member // 2, member % 2])
    chip, mine, other = gather_weights(share, place)
    recv = lax.ppermute(send, "tok", partner)

    lists = bordering_tiles[0].reshape(SHARDS, NB, KN)
    own_blocks = jnp.arange(SHARDS * NB, dtype=jnp.int32).reshape(SHARDS, NB, 1)
    named = jnp.concatenate([own_blocks, lists], axis=2).reshape(SHARDS, ITEMS)
    (target,) = call(
        target_kernel, [(1, SHARDS * PACK, jnp.int32)], (bordering_tiles[0].T,), [VM], 6 * 10**9
    )
    (packed,) = call(
        pack_kernel,
        [(SHARDS * PACK, HALF)],
        (side, target, keep, recv),
        [SM, VM, VM, VM],
        2 * SHARDS * PACK * 2 * TOK * HALF,
    )
    arrived = lax.all_to_all(
        packed.reshape(SHARDS, PACK, HALF), "tok", split_axis=0, concat_axis=0, tiled=True
    ).reshape(SHARDS * PACK, HALF)

    seen_all = unhidden_indicator[0].reshape(SHARDS, NB, BLOCK).astype(F32)
    seen_all = jnp.stack(
        [
            seen_all[:, 0],
            jnp.concatenate([seen_all[:, 1, HB:], seen_all[:, 1, :HB]], axis=1),
        ],
        axis=1,
    ).reshape(SHARDS * NB, BLOCK)
    used = jnp.arange(SLOTS)[None, :] <= bordering_tally[0][:, None]
    used = used.reshape(SHARDS, ITEMS)
    picks = (
        (named[:, :, None] == jnp.arange(SHARDS * NB)) & used[:, :, None]
    ).astype(F32)
    picks = jnp.sum(picks * (jnp.arange(SHARDS) == me)[:, None, None], axis=0)
    seen = jnp.dot(picks, seen_all).reshape(NB, KEYS)

    leaving, attended, own, out_weight = main_call(
        sharpness_coefficient,
        place,
        arrived,
        chip,
        mine,
        other,
        upstream_derivative[0],
        standardizer_multiplier.reshape(1, D),
        seen,
    )
    returned = lax.all_to_all(
        leaving.reshape(SHARDS, PACK, HALF), "tok", split_axis=0, concat_axis=0, tiled=True
    ).reshape(SHARDS * PACK, HALF)
    (layer_out,) = call(
        output_kernel,
        [(TOK, D)],
        (attended, own, out_weight),
        [VM] * 3,
        2 * TOK * HDT * D,
    )
    keep, send = call(
        collect_kernel,
        [(TOK, HALF)] * 2,
        (side, target, returned),
        [SM, VM, VM],
        2 * SHARDS * PACK * 2 * TOK * HALF,
    )
    recv = lax.ppermute(send, "tok", partner)
    (grad_tokens,) = call(
        restore_kernel,
        [(TOK, D)],
        (side, order, keep, recv),
        [SM, VM, VM, VM],
        2 * TOK * TOK * D,
    )
    return (layer_out[None], grad_tokens[None])


def solution(mesh):
    placed = (
        P("fsdp", "tok", None),
        P("fsdp", "tok", None),
        P("fsdp", None),
        P("fsdp", None, None),
        P("fsdp", None),
        P(),
        P(),
        P("fsdp", None),
        P("fsdp", None),
        P("fsdp", None),
        P(None, "fsdp"),
        P("fsdp", "tok", None),
    )
    return jax.shard_map(
        body,
        mesh=mesh,
        in_specs=placed,
        out_specs=(P("fsdp", "tok", None), P("fsdp", "tok", None)),
        check_vma=False,
    )
```

```python
import jax
import jax.numpy as jnp
from jax import lax
from jax.experimental import pallas as pl
from jax.experimental.pallas import tpu as pltpu
from jax.sharding import PartitionSpec as P

HEADS = 8
HEAD_DIM = 64
BLOCK = 64
HB = BLOCK // 2
KN = 4
D = 1024
HDT = 512
SHARDS = 32
TOK = 128
NB = 2
CHUNK = 4
SLOTS = 1 + KN
ITEMS = NB * SLOTS
ROWS = ITEMS * BLOCK
KEYS = SLOTS * BLOCK
HALF = D // 2
QB = BLOCK // 4
QROWS = ROWS // 4
FAR = ROWS + ROWS // 2
PACK = ITEMS * CHUNK
GROUP = 4
GL = GROUP * HEAD_DIM
GR = GROUP * BLOCK

CHIPS = 8
SHARE = 64
CHIP = 2 * SHARE
HOPS = 3
PARTS = 5

norm_eps = 1e-05
head_eps = 1e-06
F32 = jnp.float32
BF16 = jnp.bfloat16
VM = pl.BlockSpec(memory_space=pltpu.VMEM)
SM = pl.BlockSpec(memory_space=pltpu.SMEM)
ANY = pl.BlockSpec(memory_space=pl.ANY)
HB_SPEC = pl.BlockSpec(memory_space=pltpu.HBM)
NN = (((1,), (0,)), ((), ()))
NT = (((1,), (1,)), ((), ()))
TN = (((0,), (0,)), ((), ()))


def dot(a, b, dims, **kw):
    return lax.dot_general(a, b, dims, preferred_element_type=F32, **kw)


def rolled(m):
    return jnp.concatenate([m[:BLOCK], m[BLOCK + HB :], m[BLOCK : BLOCK + HB]], axis=0)


def split_dot(a, b, dims, which):
    exact = a if which == 0 else b
    high = exact.astype(BF16)
    low = (exact - high.astype(F32)).astype(BF16)
    if which == 0:
        return dot(high, b, dims) + dot(low, b, dims)
    return dot(a, high, dims) + dot(a, low, dims)


def one_hot(row_ref, rows):
    idx = row_ref[...]
    iota = lax.broadcasted_iota(jnp.int32, (rows, idx.shape[1]), 0)
    return jnp.where(iota == idx, 1.0, 0.0).astype(BF16)


def arrange_kernel(
    side_ref,
    order_hbm,
    x_hbm,
    wq_hbm,
    wk_hbm,
    wv_hbm,
    wo_hbm,
    keep_ref,
    send_ref,
    share_ref,
    order_ref,
    x_ref,
    sems,
):
    copies = [
        pltpu.make_async_copy(x_hbm, x_ref, sems.at[0]),
        pltpu.make_async_copy(order_hbm, order_ref, sems.at[1]),
    ]
    for n, part in enumerate((wq_hbm, wk_hbm, wv_hbm, wo_hbm)):
        lanes = pl.ds(n * HDT, HDT)
        copies.append(pltpu.make_async_copy(part, share_ref.at[:, lanes], sems.at[2 + n]))
    for copy in copies:
        copy.start()
    for copy in copies:
        copy.wait()
    a = dot(one_hot(order_ref, TOK), x_ref[...], TN).astype(BF16)
    lower = side_ref[0] == 0
    left, right = a[:, :HALF], a[:, HALF:]
    keep_ref[...] = jnp.where(lower, left, right)
    send_ref[...] = jnp.where(lower, right, left)


def stack_kernel(*refs):
    out_ref, sems = refs[-2:]
    copies, at = [], 0
    for n, ref in enumerate(refs[:-2]):
        rows = ref.shape[0]
        copies.append(pltpu.make_async_copy(ref, out_ref.at[pl.ds(at, rows), :], sems.at[n]))
        at += rows
    for copy in copies:
        copy.start()
    for copy in copies:
        copy.wait()


def pack_kernel(side_ref, target_ref, keep_ref, recv_ref, out_hbm, part_ref, sems):
    lower = side_ref[0] == 0
    keep, recv = keep_ref[...], recv_ref[...]
    table = jnp.concatenate(
        [jnp.where(lower, keep, recv), jnp.where(lower, recv, keep)], axis=0
    )
    rows = SHARDS * PACK // PARTS
    pick = one_hot(target_ref, 2 * TOK)
    copies = []
    for n in range(PARTS):
        at = slice(n * rows, (n + 1) * rows)
        part_ref[at, :] = dot(pick[:, at], table, TN).astype(BF16)
        copies.append(
            pltpu.make_async_copy(
                part_ref.at[pl.ds(n * rows, rows), :],
                out_hbm.at[pl.ds(n * rows, rows), :],
                sems.at[n],
            )
        )
        copies[-1].start()
    for copy in copies:
        copy.wait()


def collect_kernel(side_ref, target_ref, in_ref, keep_ref, send_ref):
    total = dot(one_hot(target_ref, 2 * TOK), in_ref[...], NN).astype(BF16)
    lower = side_ref[0] == 0
    even, odd = total[:TOK], total[TOK:]
    keep_ref[...] = jnp.where(lower, even, odd)
    send_ref[...] = jnp.where(lower, odd, even)


def restore_kernel(side_ref, order_ref, keep_ref, recv_ref, out_ref):
    lower = side_ref[0] == 0
    keep, recv = keep_ref[...], recv_ref[...]
    both = jnp.concatenate(
        [jnp.where(lower, keep, recv), jnp.where(lower, recv, keep)], axis=1
    )
    out_ref[...] = dot(one_hot(order_ref, TOK), both, NN).astype(BF16)


def source(dest):
    return (dest % QB // CHUNK) * PACK + (dest // QB) * CHUNK + dest % CHUNK


def quarter(q):
    right = FAR + q * QROWS if q < 2 else ROWS + (q - 2) * QROWS
    return slice(q * QROWS, (q + 1) * QROWS), slice(right, right + QROWS)


def main_kernel(
    sharp_ref,
    place_ref,
    in_ref,
    chip_any,
    mine_any,
    other_any,
    up_hbm,
    gain_ref,
    seen_ref,
    out_ref,
    att_ref,
    own_ref,
    wo_ref,
    w_ref,
    up_ref,
    sems,
    normed_ref,
    rstd_ref,
    xn_ref,
    kv_ref,
    gkv_ref,
    gq_ref,
    gh_ref,
):
    copies = [pltpu.make_async_copy(up_hbm, up_ref, sems.at[0])]

    def bring(part, at, chip, rows, first):
        chip = lax.rem(chip + CHIPS, CHIPS)
        dst = pl.ds(pl.multiple_of(chip * CHIP + first, SHARE), rows)
        src = pl.ds(at, rows)
        for lanes, ref in ((pl.ds(0, 3 * HDT), w_ref), (pl.ds(3 * HDT, HDT), wo_ref)):
            copies.append(
                pltpu.make_async_copy(part.at[src, lanes], ref.at[dst, :], sems.at[len(copies)])
            )

    y, core = place_ref[0], place_ref[1]
    bring(chip_any, 0, y, CHIP, 0)
    for part, side in ((mine_any, core), (other_any, 1 - core)):
        for hop in range(HOPS):
            bring(part, hop * CHIP, y + (2 * side - 1) * (hop + 1), CHIP, 0)
        bring(part, HOPS * CHIP, y + CHIPS // 2, SHARE, side * SHARE)
    for copy in copies:
        copy.start()
    shape = (QROWS, QROWS)
    row = source(lax.broadcasted_iota(jnp.int32, (QROWS, 1), 0))
    perm = jnp.where(row == lax.broadcasted_iota(jnp.int32, shape, 1), 1.0, 0.0).astype(BF16)
    column = source(lax.broadcasted_iota(jnp.int32, (1, QROWS), 1))
    back = jnp.where(column == lax.broadcasted_iota(jnp.int32, shape, 0), 1.0, 0.0).astype(BF16)
    for q in range(4):
        left, right = quarter(q)
        x_in = jnp.concatenate([in_ref[left, :], in_ref[right, :]], axis=1)
        x = dot(perm, x_in, NN)
        for t in range(ITEMS):
            at = t * BLOCK + q * QB
            normed_ref[at : at + QB, :] = x[t * QB : (t + 1) * QB]
    gain = gain_ref[...].astype(F32)
    for t in range(ITEMS):
        rows = pl.ds(t * BLOCK, BLOCK)
        x = normed_ref[rows, :]
        if t % SLOTS == 0:
            own_ref[pl.ds(t // SLOTS * BLOCK, BLOCK), :] = x.astype(BF16)
        centered = x - jnp.mean(x, axis=1, keepdims=True)
        rstd = 1.0 / jnp.sqrt(jnp.mean(centered * centered, axis=1, keepdims=True) + norm_eps)
        normed = centered * rstd
        normed_ref[rows, :] = normed
        rstd_ref[rows, :] = jnp.broadcast_to(rstd, (BLOCK, 128))
        xn_ref[rows, :] = (normed * gain).astype(BF16)
    for copy in copies:
        copy.wait()
    xn = xn_ref[...]
    kv_ref[...] = dot(xn, w_ref[:, HDT : 3 * HDT], NN).astype(BF16)
    xn_own = jnp.concatenate([xn_ref[pl.ds(b * KEYS, BLOCK), :] for b in range(NB)], axis=0)
    queries = dot(xn_own, w_ref[:, :HDT], NN).astype(BF16)
    up = rolled(up_ref[...])
    grad_attn = dot(up, wo_ref[...], NN).astype(BF16)

    lane_head = lax.broadcasted_iota(jnp.int32, (BLOCK, GL), 1) // HEAD_DIM
    def picks(shape):
        hit = lax.broadcasted_iota(jnp.int32, shape, 1) // HEAD_DIM == lax.broadcasted_iota(
            jnp.int32, shape, 0
        )
        return jnp.where(hit, 1.0, 0.0).astype(BF16)

    head_pick = picks((16, HDT))
    group_pick = picks((16, GL))
    diagonal = lax.broadcasted_iota(jnp.int32, (BLOCK, KEYS), 0) == lax.broadcasted_iota(
        jnp.int32, (BLOCK, KEYS), 1
    )

    def spread(m):
        return jnp.concatenate(
            [jnp.where(lane_head == h, m, jnp.zeros_like(m)) for h in range(GROUP)], axis=0
        )

    def gather_heads(m):
        total = jnp.where(lane_head == 0, m[:BLOCK], 0.0)
        for h in range(1, GROUP):
            total = jnp.where(lane_head == h, m[h * BLOCK : (h + 1) * BLOCK], total)
        return total

    for b in range(NB):
        keys = pl.ds(b * KEYS, KEYS)
        own = slice(b * BLOCK, (b + 1) * BLOCK)
        kf = kv_ref[keys, :HDT].astype(F32)
        norm2 = split_dot(head_pick, kf * kf, NT, 1)
        inv_k = 1.0 / jnp.sqrt(norm2 + head_eps)
        allowed = (seen_ref[b : b + 1, :] > 0.0) | diagonal
        mask = jnp.concatenate([allowed] * GROUP, axis=0)
        for g in range(HEADS // GROUP):
            lanes = slice(g * GL, (g + 1) * GL)
            qm = spread(queries[own, lanes])
            gm = spread(grad_attn[own, lanes])
            k4 = kv_ref[keys, lanes]
            v4 = kv_ref[keys, HDT + g * GL : HDT + (g + 1) * GL]
            qf = qm.astype(F32)
            inv_q = 1.0 / jnp.sqrt(jnp.sum(qf * qf, axis=1, keepdims=True) + head_eps)
            sharp = jnp.concatenate(
                [jnp.full((BLOCK, 1), sharp_ref[g * GROUP + h], F32) for h in range(GROUP)], axis=0
            )
            ik = inv_k[g * GROUP : (g + 1) * GROUP]
            ik_rows = jnp.concatenate(
                [jnp.broadcast_to(ik[h : h + 1], (BLOCK, KEYS)) for h in range(GROUP)], axis=0
            )
            factor = (sharp * inv_q) * ik_rows
            scores = factor * dot(qm, k4, NT)
            expo = jnp.where(mask, jnp.exp(scores), 0.0)
            prob = expo * (1.0 / jnp.sum(expo, axis=1, keepdims=True))
            prob_b = prob.astype(BF16)
            att_ref[own, lanes] = gather_heads(dot(prob_b, v4, NN)).astype(BF16)
            dprob = dot(gm, v4, NT)
            delta = jnp.sum(prob * dprob, axis=1, keepdims=True)
            dscore = prob * (dprob - delta)
            weighted = (factor * dscore).astype(BF16)
            score_grad = scores * dscore
            row_terms = jnp.sum(score_grad, axis=1, keepdims=True)
            gq = dot(weighted, k4, NN) - (inv_q * inv_q * row_terms) * qf
            gq_ref[own, lanes] = gather_heads(gq).astype(BF16)
            col_terms = jnp.concatenate(
                [
                    jnp.sum(score_grad[h * BLOCK : (h + 1) * BLOCK], axis=0, keepdims=True)
                    for h in range(GROUP)
                ],
                axis=0,
            )
            coef = ik * ik * col_terms
            coef = jnp.concatenate([coef] + [jnp.zeros_like(coef)] * 3, axis=0)
            coef = split_dot(coef, group_pick, TN, 0)
            gk = dot(weighted, qm, TN) - coef * k4.astype(F32)
            gkv_ref[keys, g * GL : (g + 1) * GL] = gk.astype(BF16)
            gkv_ref[keys, HDT + g * GL : HDT + (g + 1) * GL] = dot(prob_b, gm, TN).astype(BF16)

    gh_ref[...] = dot(gkv_ref[...], w_ref[:, HDT : 3 * HDT], NT)
    gq_hidden = dot(gq_ref[...], w_ref[:, :HDT], NT)
    for t in range(ITEMS):
        rows = pl.ds(t * BLOCK, BLOCK)
        hidden = gh_ref[rows, :]
        b = t // SLOTS
        if t % SLOTS == 0:
            hidden = hidden + gq_hidden[b * BLOCK : (b + 1) * BLOCK]
        grad = hidden * gain
        normed = normed_ref[rows, :]
        m1 = jnp.mean(grad, axis=1, keepdims=True)
        m2 = jnp.mean(grad * normed, axis=1, keepdims=True)
        grad = rstd_ref[rows, 0:1] * (grad - m1 - normed * m2)
        if t % SLOTS == 0:
            grad = grad + up[b * BLOCK : (b + 1) * BLOCK].astype(F32)
        xn_ref[rows, :] = grad.astype(BF16)
    for q in range(4):
        left, right = quarter(q)
        x = jnp.concatenate(
            [xn_ref[t * BLOCK + q * QB : t * BLOCK + (q + 1) * QB, :] for t in range(ITEMS)], axis=0
        )
        x = dot(back, x, NN).astype(BF16)
        out_ref[left, :] = x[:, :HALF]
        out_ref[right, :] = x[:, HALF:]


def output_kernel(att_ref, own_ref, wo_ref, out_ref):
    out = own_ref[...].astype(F32) + dot(att_ref[...], wo_ref[...], NT)
    out_ref[...] = rolled(out.astype(BF16))


def call(kernel, outs, args, specs, flops, scratch=(), limit=8, out_spec=VM):
    place = pltpu.HBM if out_spec is HB_SPEC else jax.ShapeDtypeStruct
    moved = sum(a.size * a.dtype.itemsize for a in args)
    moved += sum(2 * o[0] * o[1] for o in outs)
    if flops == 0:
        moved = 0
    args = [
        pltpu.with_memory_space_constraint(a, pltpu.HBM) if spec is HB_SPEC else a
        for a, spec in zip(args, specs)
    ]
    return pl.pallas_call(
        kernel,
        out_shape=[place(o[:2], o[2] if len(o) > 2 else BF16) for o in outs],
        in_specs=specs,
        out_specs=[out_spec] * len(outs),
        scratch_shapes=list(scratch),
        compiler_params=pltpu.CompilerParams(vmem_limit_bytes=limit * 2**20),
        cost_estimate=pl.CostEstimate(flops=flops, bytes_accessed=moved, transcendentals=0),
    )(*args)


def gather_weights(share, place):
    members = 2 * CHIPS
    sibling = [(i, i ^ 1) for i in range(members)]

    def onward(part, hops):
        pairs = [(i, (i + hops * (2 - 4 * (i % 2))) % members) for i in range(members)]
        return lax.ppermute(part, "fsdp", pairs)

    first = place[1] == 0
    beside = lax.ppermute(share, "fsdp", sibling)
    chip = jnp.concatenate(
        [jnp.where(first, share, beside), jnp.where(first, beside, share)], axis=0
    )
    near, far = onward(chip, 1), onward(chip, 2)
    half = jnp.where(first, far[:SHARE], far[SHARE:])
    pieces = [near, far, onward(far, 1), onward(half, 2)]
    (mine,) = call(
        stack_kernel,
        [(HOPS * CHIP + SHARE, 4 * HDT)],
        pieces,
        [HB_SPEC] * (HOPS + 1),
        0,
        scratch=[pltpu.SemaphoreType.DMA((HOPS + 1,))],
    )
    return chip, mine, lax.ppermute(mine, "fsdp", sibling)


def main_call(sharpness_coefficient, place, arrived, chip, mine, other, upstream_derivative, gain, seen):
    return call(
        main_kernel,
        [(SHARDS * PACK, HALF), (TOK, HDT), (TOK, D), (D, HDT)],
        (
            sharpness_coefficient,
            place,
            arrived,
            chip,
            mine,
            other,
            upstream_derivative,
            gain,
            seen,
        ),
        [SM, SM, VM, HB_SPEC, ANY, ANY, HB_SPEC, VM, VM],
        4 * 10**9,
        scratch=[
            pltpu.VMEM((D, 3 * HDT), BF16),
            pltpu.VMEM((TOK, D), BF16),
            pltpu.SemaphoreType.DMA((7 + 4 * (HOPS + 1),)),
            pltpu.VMEM((ROWS, D), F32),
            pltpu.VMEM((ROWS, 128), F32),
            pltpu.VMEM((ROWS, D), BF16),
            pltpu.VMEM((ROWS, D), BF16),
            pltpu.VMEM((ROWS, D), BF16),
            pltpu.VMEM((TOK, HDT), BF16),
            pltpu.VMEM((ROWS, D), F32),
        ],
        limit=40,
    )


def body(
    embedded_pieces,
    morton_arrangement,
    unhidden_indicator,
    bordering_tiles,
    bordering_tally,
    standardizer_multiplier,
    sharpness_coefficient,
    probe_projector,
    lookup_projector,
    content_projector,
    result_projector,
    upstream_derivative,
):
    me = lax.axis_index("tok")
    side = (me // (SHARDS // 2)).reshape(1).astype(jnp.int32)
    column = SHARDS // 4
    partner = [(i, (3 - i // column) * column + i % column) for i in range(SHARDS)]

    order = morton_arrangement[0]
    keep, send, share = call(
        arrange_kernel,
        [(TOK, HALF)] * 2 + [(SHARE, 4 * HDT)],
        (
            side,
            order,
            embedded_pieces[0],
            probe_projector,
            lookup_projector,
            content_projector,
            result_projector.T,
        ),
        [SM] + [HB_SPEC] * 6,
        2 * TOK * TOK * D,
        scratch=[
            pltpu.VMEM((1, TOK), jnp.int32),
            pltpu.VMEM((TOK, D), BF16),
            pltpu.SemaphoreType.DMA((6,)),
        ],
    )
    member = lax.axis_index("fsdp").astype(jnp.int32)
    place = jnp.stack([member // 2, member % 2])
    chip, mine, other = gather_weights(share, place)
    recv = lax.ppermute(send, "tok", partner)

    lists = bordering_tiles[0].reshape(SHARDS, NB, KN)
    own_blocks = jnp.arange(SHARDS * NB, dtype=jnp.int32).reshape(SHARDS, NB, 1)
    named = jnp.concatenate([own_blocks, lists], axis=2).reshape(SHARDS, ITEMS)
    target = (named % 2) * TOK + (named // 2) * CHUNK
    target = (target[:, :, None] + jnp.arange(CHUNK, dtype=jnp.int32)).reshape(
        1, SHARDS * PACK
    )
    (packed,) = call(
        pack_kernel,
        [(SHARDS * PACK, HALF)],
        (side, target, keep, recv),
        [SM, VM, VM, VM],
        2 * SHARDS * PACK * 2 * TOK * HALF,
        scratch=[
            pltpu.VMEM((SHARDS * PACK, HALF), BF16),
            pltpu.SemaphoreType.DMA((PARTS,)),
        ],
        out_spec=HB_SPEC,
    )
    arrived = lax.all_to_all(
        packed.reshape(SHARDS, PACK, HALF), "tok", split_axis=0, concat_axis=0, tiled=True
    ).reshape(SHARDS * PACK, HALF)

    seen_all = unhidden_indicator[0].reshape(SHARDS, NB, BLOCK).astype(F32)
    seen_all = jnp.stack(
        [
            seen_all[:, 0],
            jnp.concatenate([seen_all[:, 1, HB:], seen_all[:, 1, :HB]], axis=1),
        ],
        axis=1,
    ).reshape(SHARDS * NB, BLOCK)
    used = jnp.arange(SLOTS)[None, :] <= bordering_tally[0][:, None]
    used = used.reshape(SHARDS, ITEMS)
    picks = (
        (named[:, :, None] == jnp.arange(SHARDS * NB)) & used[:, :, None]
    ).astype(F32)
    picks = jnp.sum(picks * (jnp.arange(SHARDS) == me)[:, None, None], axis=0)
    seen = jnp.dot(picks, seen_all).reshape(NB, KEYS)

    leaving, attended, own, out_weight = main_call(
        sharpness_coefficient,
        place,
        arrived,
        chip,
        mine,
        other,
        upstream_derivative[0],
        standardizer_multiplier.reshape(1, D),
        seen,
    )
    returned = lax.all_to_all(
        leaving.reshape(SHARDS, PACK, HALF), "tok", split_axis=0, concat_axis=0, tiled=True
    ).reshape(SHARDS * PACK, HALF)
    (layer_out,) = call(
        output_kernel,
        [(TOK, D)],
        (attended, own, out_weight),
        [VM] * 3,
        2 * TOK * HDT * D,
    )
    keep, send = call(
        collect_kernel,
        [(TOK, HALF)] * 2,
        (side, target, returned),
        [SM, VM, VM],
        2 * SHARDS * PACK * 2 * TOK * HALF,
    )
    recv = lax.ppermute(send, "tok", partner)
    (grad_tokens,) = call(
        restore_kernel,
        [(TOK, D)],
        (side, order, keep, recv),
        [SM, VM, VM, VM],
        2 * TOK * TOK * D,
    )
    return (layer_out[None], grad_tokens[None])


def solution(mesh):
    placed = (
        P("fsdp", "tok", None),
        P("fsdp", "tok", None),
        P("fsdp", None),
        P("fsdp", None, None),
        P("fsdp", None),
        P(),
        P(),
        P("fsdp", None),
        P("fsdp", None),
        P("fsdp", None),
        P(None, "fsdp"),
        P("fsdp", "tok", None),
    )
    return jax.shard_map(
        body,
        mesh=mesh,
        in_specs=placed,
        out_specs=(P("fsdp", "tok", None), P("fsdp", "tok", None)),
        check_vma=False,
    )
```

```python
import jax
import jax.numpy as jnp
from jax import lax
from jax.experimental import pallas as pl
from jax.experimental.pallas import tpu as pltpu
from jax.sharding import PartitionSpec as P

HEADS = 8
HEAD_DIM = 64
BLOCK = 64
HB = BLOCK // 2
KN = 4
D = 1024
HDT = 512
SHARDS = 32
TOK = 128
NB = 2
CHUNK = 4
SLOTS = 1 + KN
ITEMS = NB * SLOTS
ROWS = ITEMS * BLOCK
KEYS = SLOTS * BLOCK
HALF = D // 2
QB = BLOCK // 4
QROWS = ROWS // 4
FAR = ROWS + ROWS // 2
PACK = ITEMS * CHUNK
GROUP = 4
GL = GROUP * HEAD_DIM
GR = GROUP * BLOCK

CHIPS = 8
SHARE = 64
CHIP = 2 * SHARE
HOPS = 3

norm_eps = 1e-05
head_eps = 1e-06
F32 = jnp.float32
BF16 = jnp.bfloat16
VM = pl.BlockSpec(memory_space=pltpu.VMEM)
SM = pl.BlockSpec(memory_space=pltpu.SMEM)
ANY = pl.BlockSpec(memory_space=pl.ANY)
HB_SPEC = pl.BlockSpec(memory_space=pltpu.HBM)
NN = (((1,), (0,)), ((), ()))
NT = (((1,), (1,)), ((), ()))
TN = (((0,), (0,)), ((), ()))


def dot(a, b, dims, **kw):
    return lax.dot_general(a, b, dims, preferred_element_type=F32, **kw)


def rolled(m):
    return jnp.concatenate([m[:BLOCK], m[BLOCK + HB :], m[BLOCK : BLOCK + HB]], axis=0)


def split_dot(a, b, dims, which):
    exact = a if which == 0 else b
    high = exact.astype(BF16)
    low = (exact - high.astype(F32)).astype(BF16)
    if which == 0:
        return dot(high, b, dims) + dot(low, b, dims)
    return dot(a, high, dims) + dot(a, low, dims)


def one_hot(row_ref, rows):
    idx = row_ref[...]
    iota = lax.broadcasted_iota(jnp.int32, (rows, idx.shape[1]), 0)
    return jnp.where(iota == idx, 1.0, 0.0).astype(BF16)


def arrange_kernel(
    side_ref,
    order_hbm,
    x_hbm,
    wq_hbm,
    wk_hbm,
    wv_hbm,
    wo_hbm,
    keep_ref,
    send_ref,
    share_ref,
    order_ref,
    x_ref,
    sems,
):
    copies = [
        pltpu.make_async_copy(x_hbm, x_ref, sems.at[0]),
        pltpu.make_async_copy(order_hbm, order_ref, sems.at[1]),
    ]
    for n, part in enumerate((wq_hbm, wk_hbm, wv_hbm, wo_hbm)):
        lanes = pl.ds(n * HDT, HDT)
        copies.append(pltpu.make_async_copy(part, share_ref.at[:, lanes], sems.at[2 + n]))
    for copy in copies:
        copy.start()
    for copy in copies:
        copy.wait()
    a = dot(one_hot(order_ref, TOK), x_ref[...], TN).astype(BF16)
    lower = side_ref[0] == 0
    left, right = a[:, :HALF], a[:, HALF:]
    keep_ref[...] = jnp.where(lower, left, right)
    send_ref[...] = jnp.where(lower, right, left)


def stack_kernel(*refs):
    out_ref, sems = refs[-2:]
    copies, at = [], 0
    for n, ref in enumerate(refs[:-2]):
        rows = ref.shape[0]
        copies.append(pltpu.make_async_copy(ref, out_ref.at[pl.ds(at, rows), :], sems.at[n]))
        at += rows
    for copy in copies:
        copy.start()
    for copy in copies:
        copy.wait()


def pack_kernel(side_ref, target_ref, keep_ref, recv_ref, out_ref):
    lower = side_ref[0] == 0
    keep, recv = keep_ref[...], recv_ref[...]
    table = jnp.concatenate(
        [jnp.where(lower, keep, recv), jnp.where(lower, recv, keep)], axis=0
    )
    out_ref[...] = dot(one_hot(target_ref, 2 * TOK), table, TN).astype(BF16)


def collect_kernel(side_ref, target_ref, in_ref, keep_ref, send_ref):
    total = dot(one_hot(target_ref, 2 * TOK), in_ref[...], NN).astype(BF16)
    lower = side_ref[0] == 0
    even, odd = total[:TOK], total[TOK:]
    keep_ref[...] = jnp.where(lower, even, odd)
    send_ref[...] = jnp.where(lower, odd, even)


def restore_kernel(side_ref, order_ref, keep_ref, recv_ref, out_ref):
    lower = side_ref[0] == 0
    keep, recv = keep_ref[...], recv_ref[...]
    both = jnp.concatenate(
        [jnp.where(lower, keep, recv), jnp.where(lower, recv, keep)], axis=1
    )
    out_ref[...] = dot(one_hot(order_ref, TOK), both, NN).astype(BF16)


def source(dest):
    return (dest % QB // CHUNK) * PACK + (dest // QB) * CHUNK + dest % CHUNK


def quarter(q):
    right = FAR + q * QROWS if q < 2 else ROWS + (q - 2) * QROWS
    return slice(q * QROWS, (q + 1) * QROWS), slice(right, right + QROWS)


def main_kernel(
    sharp_ref,
    place_ref,
    in_ref,
    chip_any,
    mine_any,
    other_any,
    up_hbm,
    gain_ref,
    seen_ref,
    out_ref,
    att_ref,
    own_ref,
    wo_ref,
    w_ref,
    up_ref,
    sems,
    normed_ref,
    rstd_ref,
    xn_ref,
    k_ref,
    v_ref,
    gkv_ref,
    gq_ref,
    gh_ref,
):
    copies = [pltpu.make_async_copy(up_hbm, up_ref, sems.at[0])]

    def bring(part, at, chip, rows, first):
        chip = lax.rem(chip + CHIPS, CHIPS)
        dst = pl.ds(pl.multiple_of(chip * CHIP + first, SHARE), rows)
        src = pl.ds(at, rows)
        for lanes, ref in ((pl.ds(0, 3 * HDT), w_ref), (pl.ds(3 * HDT, HDT), wo_ref)):
            copies.append(
                pltpu.make_async_copy(part.at[src, lanes], ref.at[dst, :], sems.at[len(copies)])
            )

    y, core = place_ref[0], place_ref[1]
    bring(chip_any, 0, y, CHIP, 0)
    for part, side in ((mine_any, core), (other_any, 1 - core)):
        for hop in range(HOPS):
            bring(part, hop * CHIP, y + (2 * side - 1) * (hop + 1), CHIP, 0)
        bring(part, HOPS * CHIP, y + CHIPS // 2, SHARE, side * SHARE)
    for copy in copies:
        copy.start()
    shape = (QROWS, QROWS)
    row = source(lax.broadcasted_iota(jnp.int32, (QROWS, 1), 0))
    perm = jnp.where(row == lax.broadcasted_iota(jnp.int32, shape, 1), 1.0, 0.0).astype(BF16)
    column = source(lax.broadcasted_iota(jnp.int32, (1, QROWS), 1))
    back = jnp.where(column == lax.broadcasted_iota(jnp.int32, shape, 0), 1.0, 0.0).astype(BF16)
    for q in range(4):
        left, right = quarter(q)
        x_in = jnp.concatenate([in_ref[left, :], in_ref[right, :]], axis=1)
        x = dot(perm, x_in, NN)
        for t in range(ITEMS):
            at = t * BLOCK + q * QB
            normed_ref[at : at + QB, :] = x[t * QB : (t + 1) * QB]
    gain = gain_ref[...].astype(F32)
    for t in range(ITEMS):
        rows = pl.ds(t * BLOCK, BLOCK)
        x = normed_ref[rows, :]
        if t % SLOTS == 0:
            own_ref[pl.ds(t // SLOTS * BLOCK, BLOCK), :] = x.astype(BF16)
        centered = x - jnp.mean(x, axis=1, keepdims=True)
        rstd = 1.0 / jnp.sqrt(jnp.mean(centered * centered, axis=1, keepdims=True) + norm_eps)
        normed = centered * rstd
        normed_ref[rows, :] = normed
        rstd_ref[rows, :] = jnp.broadcast_to(rstd, (BLOCK, 128))
        xn_ref[rows, :] = (normed * gain).astype(BF16)
    for copy in copies:
        copy.wait()
    xn = xn_ref[...]
    k_ref[...] = dot(xn, w_ref[:, HDT : 2 * HDT], NN).astype(BF16)
    v_ref[...] = dot(xn, w_ref[:, 2 * HDT : 3 * HDT], NN).astype(BF16)
    xn_own = jnp.concatenate([xn_ref[pl.ds(b * KEYS, BLOCK), :] for b in range(NB)], axis=0)
    queries = dot(xn_own, w_ref[:, :HDT], NN).astype(BF16)
    up = rolled(up_ref[...])
    grad_attn = dot(up, wo_ref[...], NN).astype(BF16)

    lane_head = lax.broadcasted_iota(jnp.int32, (BLOCK, GL), 1) // HEAD_DIM
    def picks(shape):
        hit = lax.broadcasted_iota(jnp.int32, shape, 1) // HEAD_DIM == lax.broadcasted_iota(
            jnp.int32, shape, 0
        )
        return jnp.where(hit, 1.0, 0.0).astype(BF16)

    head_pick = picks((16, HDT))
    group_pick = picks((16, GL))
    diagonal = lax.broadcasted_iota(jnp.int32, (BLOCK, KEYS), 0) == lax.broadcasted_iota(
        jnp.int32, (BLOCK, KEYS), 1
    )

    def spread(m):
        return jnp.concatenate(
            [jnp.where(lane_head == h, m, jnp.zeros_like(m)) for h in range(GROUP)], axis=0
        )

    def gather_heads(m):
        total = jnp.where(lane_head == 0, m[:BLOCK], 0.0)
        for h in range(1, GROUP):
            total = jnp.where(lane_head == h, m[h * BLOCK : (h + 1) * BLOCK], total)
        return total

    for b in range(NB):
        keys = pl.ds(b * KEYS, KEYS)
        own = slice(b * BLOCK, (b + 1) * BLOCK)
        kf = k_ref[keys, :].astype(F32)
        norm2 = split_dot(head_pick, kf * kf, NT, 1)
        inv_k = 1.0 / jnp.sqrt(norm2 + head_eps)
        allowed = (seen_ref[b : b + 1, :] > 0.0) | diagonal
        mask = jnp.concatenate([allowed] * GROUP, axis=0)
        for g in range(HEADS // GROUP):
            lanes = slice(g * GL, (g + 1) * GL)
            qm = spread(queries[own, lanes])
            gm = spread(grad_attn[own, lanes])
            k4 = k_ref[keys, lanes]
            v4 = v_ref[keys, lanes]
            qf = qm.astype(F32)
            inv_q = 1.0 / jnp.sqrt(jnp.sum(qf * qf, axis=1, keepdims=True) + head_eps)
            sharp = jnp.concatenate(
                [jnp.full((BLOCK, 1), sharp_ref[g * GROUP + h], F32) for h in range(GROUP)], axis=0
            )
            ik = inv_k[g * GROUP : (g + 1) * GROUP]
            ik_rows = jnp.concatenate(
                [jnp.broadcast_to(ik[h : h + 1], (BLOCK, KEYS)) for h in range(GROUP)], axis=0
            )
            factor = (sharp * inv_q) * ik_rows
            scores = factor * dot(qm, k4, NT)
            expo = jnp.where(mask, jnp.exp(scores), 0.0)
            prob = expo * (1.0 / jnp.sum(expo, axis=1, keepdims=True))
            prob_b = prob.astype(BF16)
            att_ref[own, lanes] = gather_heads(dot(prob_b, v4, NN)).astype(BF16)
            dprob = dot(gm, v4, NT)
            delta = jnp.sum(prob * dprob, axis=1, keepdims=True)
            dscore = prob * (dprob - delta)
            weighted = (factor * dscore).astype(BF16)
            score_grad = scores * dscore
            row_terms = jnp.sum(score_grad, axis=1, keepdims=True)
            gq = dot(weighted, k4, NN) - (inv_q * inv_q * row_terms) * qf
            gq_ref[own, lanes] = gather_heads(gq).astype(BF16)
            col_terms = jnp.concatenate(
                [
                    jnp.sum(score_grad[h * BLOCK : (h + 1) * BLOCK], axis=0, keepdims=True)
                    for h in range(GROUP)
                ],
                axis=0,
            )
            coef = ik * ik * col_terms
            coef = jnp.concatenate([coef] + [jnp.zeros_like(coef)] * 3, axis=0)
            coef = split_dot(coef, group_pick, TN, 0)
            gk = dot(weighted, qm, TN) - coef * k4.astype(F32)
            gkv_ref[keys, g * GL : (g + 1) * GL] = gk.astype(BF16)
            gkv_ref[keys, HDT + g * GL : HDT + (g + 1) * GL] = dot(prob_b, gm, TN).astype(BF16)

    gh_ref[...] = dot(gkv_ref[...], w_ref[:, HDT : 3 * HDT], NT)
    gq_hidden = dot(gq_ref[...], w_ref[:, :HDT], NT)
    for t in range(ITEMS):
        rows = pl.ds(t * BLOCK, BLOCK)
        hidden = gh_ref[rows, :]
        b = t // SLOTS
        if t % SLOTS == 0:
            hidden = hidden + gq_hidden[b * BLOCK : (b + 1) * BLOCK]
        grad = hidden * gain
        normed = normed_ref[rows, :]
        m1 = jnp.mean(grad, axis=1, keepdims=True)
        m2 = jnp.mean(grad * normed, axis=1, keepdims=True)
        grad = rstd_ref[rows, 0:1] * (grad - m1 - normed * m2)
        if t % SLOTS == 0:
            grad = grad + up[b * BLOCK : (b + 1) * BLOCK].astype(F32)
        xn_ref[rows, :] = grad.astype(BF16)
    for q in range(4):
        left, right = quarter(q)
        x = jnp.concatenate(
            [xn_ref[t * BLOCK + q * QB : t * BLOCK + (q + 1) * QB, :] for t in range(ITEMS)], axis=0
        )
        x = dot(back, x, NN).astype(BF16)
        out_ref[left, :] = x[:, :HALF]
        out_ref[right, :] = x[:, HALF:]


def output_kernel(att_ref, own_ref, wo_ref, out_ref):
    out = own_ref[...].astype(F32) + dot(att_ref[...], wo_ref[...], NT)
    out_ref[...] = rolled(out.astype(BF16))


def call(kernel, outs, args, specs, flops, scratch=(), limit=8, out_spec=VM):
    place = pltpu.HBM if out_spec is HB_SPEC else jax.ShapeDtypeStruct
    moved = sum(a.size * a.dtype.itemsize for a in args)
    moved += sum(2 * o[0] * o[1] for o in outs)
    if flops == 0:
        moved = 0
    args = [
        pltpu.with_memory_space_constraint(a, pltpu.HBM) if spec is HB_SPEC else a
        for a, spec in zip(args, specs)
    ]
    return pl.pallas_call(
        kernel,
        out_shape=[place(o[:2], o[2] if len(o) > 2 else BF16) for o in outs],
        in_specs=specs,
        out_specs=[out_spec] * len(outs),
        scratch_shapes=list(scratch),
        compiler_params=pltpu.CompilerParams(vmem_limit_bytes=limit * 2**20),
        cost_estimate=pl.CostEstimate(flops=flops, bytes_accessed=moved, transcendentals=0),
    )(*args)


def gather_weights(share, place, recv):
    members = 2 * CHIPS
    sibling = [(i, i ^ 1) for i in range(members)]

    def onward(part, hops):
        pairs = [(i, (i + hops * (2 - 4 * (i % 2))) % members) for i in range(members)]
        return lax.ppermute(part, "fsdp", pairs)

    first = place[1] == 0
    beside = lax.ppermute(share, "fsdp", sibling)
    chip = jnp.concatenate(
        [jnp.where(first, share, beside), jnp.where(first, beside, share)], axis=0
    )
    chip, recv = lax.optimization_barrier((chip, recv))
    near, far = onward(chip, 1), onward(chip, 2)
    half = jnp.where(first, far[:SHARE], far[SHARE:])
    pieces = [near, far, onward(far, 1), onward(half, 2)]
    (mine,) = call(
        stack_kernel,
        [(HOPS * CHIP + SHARE, 4 * HDT)],
        pieces,
        [HB_SPEC] * (HOPS + 1),
        0,
        scratch=[pltpu.SemaphoreType.DMA((HOPS + 1,))],
    )
    return chip, mine, lax.ppermute(mine, "fsdp", sibling), recv


def main_call(sharpness_coefficient, place, arrived, chip, mine, other, upstream_derivative, gain, seen):
    return call(
        main_kernel,
        [(SHARDS * PACK, HALF), (TOK, HDT), (TOK, D), (D, HDT)],
        (
            sharpness_coefficient,
            place,
            arrived,
            chip,
            mine,
            other,
            upstream_derivative,
            gain,
            seen,
        ),
        [SM, SM, VM, HB_SPEC, ANY, ANY, HB_SPEC, VM, VM],
        4 * 10**9,
        scratch=[
            pltpu.VMEM((D, 3 * HDT), BF16),
            pltpu.VMEM((TOK, D), BF16),
            pltpu.SemaphoreType.DMA((7 + 4 * (HOPS + 1),)),
            pltpu.VMEM((ROWS, D), F32),
            pltpu.VMEM((ROWS, 128), F32),
            pltpu.VMEM((ROWS, D), BF16),
            pltpu.VMEM((ROWS, HDT), BF16),
            pltpu.VMEM((ROWS, HDT), BF16),
            pltpu.VMEM((ROWS, D), BF16),
            pltpu.VMEM((TOK, HDT), BF16),
            pltpu.VMEM((ROWS, D), F32),
        ],
        limit=40,
    )


def body(
    embedded_pieces,
    morton_arrangement,
    unhidden_indicator,
    bordering_tiles,
    bordering_tally,
    standardizer_multiplier,
    sharpness_coefficient,
    probe_projector,
    lookup_projector,
    content_projector,
    result_projector,
    upstream_derivative,
):
    me = lax.axis_index("tok")
    side = (me // (SHARDS // 2)).reshape(1).astype(jnp.int32)
    column = SHARDS // 4
    partner = [(i, (3 - i // column) * column + i % column) for i in range(SHARDS)]

    order = morton_arrangement[0]
    keep, send, share = call(
        arrange_kernel,
        [(TOK, HALF)] * 2 + [(SHARE, 4 * HDT)],
        (
            side,
            order,
            embedded_pieces[0],
            probe_projector,
            lookup_projector,
            content_projector,
            result_projector.T,
        ),
        [SM] + [HB_SPEC] * 6,
        2 * TOK * TOK * D,
        scratch=[
            pltpu.VMEM((1, TOK), jnp.int32),
            pltpu.VMEM((TOK, D), BF16),
            pltpu.SemaphoreType.DMA((6,)),
        ],
    )
    member = lax.axis_index("fsdp").astype(jnp.int32)
    place = jnp.stack([member // 2, member % 2])
    recv = lax.ppermute(send, "tok", partner)
    chip, mine, other, recv = gather_weights(share, place, recv)

    lists = bordering_tiles[0].reshape(SHARDS, NB, KN)
    own_blocks = jnp.arange(SHARDS * NB, dtype=jnp.int32).reshape(SHARDS, NB, 1)
    named = jnp.concatenate([own_blocks, lists], axis=2).reshape(SHARDS, ITEMS)
    target = (named % 2) * TOK + (named // 2) * CHUNK
    target = (target[:, :, None] + jnp.arange(CHUNK, dtype=jnp.int32)).reshape(
        1, SHARDS * PACK
    )
    (packed,) = call(
        pack_kernel,
        [(SHARDS * PACK, HALF)],
        (side, target, keep, recv),
        [SM, VM, VM, VM],
        2 * SHARDS * PACK * 2 * TOK * HALF,
    )
    arrived = lax.all_to_all(
        packed.reshape(SHARDS, PACK, HALF), "tok", split_axis=0, concat_axis=0, tiled=True
    ).reshape(SHARDS * PACK, HALF)

    seen_all = unhidden_indicator[0].reshape(SHARDS, NB, BLOCK).astype(F32)
    seen_all = jnp.stack(
        [
            seen_all[:, 0],
            jnp.concatenate([seen_all[:, 1, HB:], seen_all[:, 1, :HB]], axis=1),
        ],
        axis=1,
    ).reshape(SHARDS * NB, BLOCK)
    used = jnp.arange(SLOTS)[None, :] <= bordering_tally[0][:, None]
    used = used.reshape(SHARDS, ITEMS)
    picks = (
        (named[:, :, None] == jnp.arange(SHARDS * NB)) & used[:, :, None]
    ).astype(F32)
    picks = jnp.sum(picks * (jnp.arange(SHARDS) == me)[:, None, None], axis=0)
    seen = jnp.dot(picks, seen_all).reshape(NB, KEYS)

    leaving, attended, own, out_weight = main_call(
        sharpness_coefficient,
        place,
        arrived,
        chip,
        mine,
        other,
        upstream_derivative[0],
        standardizer_multiplier.reshape(1, D),
        seen,
    )
    returned = lax.all_to_all(
        leaving.reshape(SHARDS, PACK, HALF), "tok", split_axis=0, concat_axis=0, tiled=True
    ).reshape(SHARDS * PACK, HALF)
    (layer_out,) = call(
        output_kernel,
        [(TOK, D)],
        (attended, own, out_weight),
        [VM] * 3,
        2 * TOK * HDT * D,
    )
    keep, send = call(
        collect_kernel,
        [(TOK, HALF)] * 2,
        (side, target, returned),
        [SM, VM, VM],
        2 * SHARDS * PACK * 2 * TOK * HALF,
    )
    recv = lax.ppermute(send, "tok", partner)
    (grad_tokens,) = call(
        restore_kernel,
        [(TOK, D)],
        (side, order, keep, recv),
        [SM, VM, VM, VM],
        2 * TOK * TOK * D,
    )
    return (layer_out[None], grad_tokens[None])


def solution(mesh):
    placed = (
        P("fsdp", "tok", None),
        P("fsdp", "tok", None),
        P("fsdp", None),
        P("fsdp", None, None),
        P("fsdp", None),
        P(),
        P(),
        P("fsdp", None),
        P("fsdp", None),
        P("fsdp", None),
        P(None, "fsdp"),
        P("fsdp", "tok", None),
    )
    return jax.shard_map(
        body,
        mesh=mesh,
        in_specs=placed,
        out_specs=(P("fsdp", "tok", None), P("fsdp", "tok", None)),
        check_vma=False,
    )
```
